512 devices in a mesh: gx: 32 (over x_hi, z), gy: 16 (over x_lo, y, core).
Axes of the slice: x: 4 (x_hi: 2, x_lo: 2; x = x_hi * 2 + x_lo), y: 4, z: 16, core: 2. Of those that a mesh axis runs over, the one named last changes fastest.
Arguments:
- matrix: float32 [262144, 512], P(('gx', 'gy'))
- signs: int32 [262144], P(('gx', 'gy')), may hold values from -1 to 1, as said below
- samples: int32 [2048], replicated, may hold values from 0 to 262143, as said below
Outputs:
- factor: float32 [512, 512], replicated
- preconditioned: float32 [262144, 512], P(('gx', 'gy'))
The draws below stay inside these ranges and needn't reach their ends.
Inputs may be any that keep to these rules, and one draw needn't show every extreme that they name: `signs`: each entry is +1 or -1. `samples`: row indices drawn with replacement; may repeat.
All inputs are finite; a program needn't handle non-finite values.
Results may differ from the reference program's by a relative error of at most 0.00012.
Values sent between devices are 32-bit elements; how exact they have to be, the bound alone decides.
No kernel may reach another device: no remote copies, remote signals or barrier semaphores. Data moves between devices by JAX's collectives and lax.ppermute only.
A program may use at most 64 MiB of HBM per device.

```python
import math
import jax
import jax.numpy as jnp
from jax import lax

N = 512
SAMPLES = 2048
ROWS = 262144


def draw_matrix(key, part):
    key = jax.random.fold_in(key, 11)
    first, second, third = jax.random.split(key, 3)
    ramp = 1.0 + 2.0 * jnp.arange(ROWS, dtype=jnp.float32)[:, None] / ROWS
    row_scale = jnp.exp(jax.random.uniform(second, (ROWS, 1)) * math.log(10.0)) * ramp
    col_scale = jnp.exp(jax.random.uniform(third, (1, N)) * math.log(10.0))
    base = jax.random.normal(first, (ROWS, N))
    return (0.1 * base * row_scale * col_scale).astype(jnp.float32)


def draw_signs(key, part):
    key = jax.random.fold_in(key, 23)
    return (2 * jax.random.randint(key, (ROWS,), 0, 2) - 1).astype(jnp.int32)


def draw_samples(key, part):
    key = jax.random.fold_in(key, 37)
    picked = jax.random.randint(key, (SAMPLES,), 0, ROWS)
    picked = picked.at[0].set(ROWS - 1).at[1].set(0)
    return picked.astype(jnp.int32)


def setup_inputs(seed: int = 0) -> dict:
    keys = jax.random.split(jax.random.key(seed), 4)
    matrix = draw_matrix(jax.random.fold_in(keys[3], 71), 0)
    signs = draw_signs(jax.random.fold_in(keys[3], 71), 0)
    samples = draw_samples(jax.random.fold_in(keys[3], 71), 0)
    return {"matrix": matrix, "signs": signs, "samples": samples}


def reference(matrix, signs, samples):
    mixed = signs.astype(jnp.float32)[:, None] * matrix
    width = matrix.shape[1]
    half = 1
    while half < ROWS:
        blocks = mixed.reshape(ROWS // (2 * half), 2, half, width)
        upper = blocks[:, 0]
        lower = blocks[:, 1]
        mixed = jnp.stack([upper + lower, upper - lower], axis=1).reshape(ROWS, width)
        half = half * 2
    mixed = mixed / jnp.sqrt(jnp.float32(ROWS))
    picked = jnp.take(mixed, samples, axis=0)
    gram = jnp.dot(picked.T, picked, precision=lax.Precision.HIGHEST) / jnp.float32(SAMPLES)
    factor = jnp.linalg.cholesky(gram)
    solved = jax.scipy.linalg.solve_triangular(factor, matrix.T, lower=True)
    return (factor, solved.T)
```

```python
import jax
import jax.numpy as jnp
from jax import lax
from jax.experimental import pallas as pl
from jax.experimental.pallas import tpu as pltpu
from jax.sharding import Mesh
from jax.sharding import PartitionSpec as P

BLOCK = 128
PANEL = 8
CHUNK = 256
ROW_AXES = ("x_hi", "z", "x_lo", "y", "core")
PLANE = ("x_hi", "x_lo", "y", "core")
NN = ((1,), (0,))
NT = ((1,), (1,))


def split2(x):
    hi = x.astype(jnp.bfloat16)
    lo = (x - hi.astype(jnp.float32)).astype(jnp.bfloat16)
    return hi, lo


def dot3(a, b, dims):
    (ah, al), (bh, bl) = a, b
    dg = lambda p, q: lax.dot_general(p, q, (dims, ((), ())), preferred_element_type=jnp.float32)
    return dg(ah, bh) + (dg(ah, bl) + dg(al, bh))


def factor_block(rows):
    count = len(rows)
    lane = lax.broadcasted_iota(jnp.int32, (PANEL, BLOCK), 1)
    sub = lax.broadcasted_iota(jnp.int32, (PANEL, BLOCK), 0)
    rows = list(rows)
    upper, inverse = [], []
    full = (PANEL, BLOCK)
    for k in range(count):
        base = k * PANEL
        own = (lane >= base) & (lane < base + PANEL)
        panel = rows[k]
        piv = {}
        for j in range(PANEL):
            col = jnp.broadcast_to(panel[:, base + j : base + j + 1], full)
            for i in range(j, PANEL):
                piv[i, j] = jnp.broadcast_to(col[i : i + 1, :], full)
        cols = {}
        for r in range(k + 1, count):
            for j in range(PANEL):
                cols[r, j] = jnp.broadcast_to(rows[r][:, base + j : base + j + 1], full)
        root, inv, low = [], [], {}
        for j in range(PANEL):
            s = lax.rsqrt(piv[j, j])
            root.append(s)
            d = s * s
            inv.append(d)
            for i in range(j + 1, PANEL):
                low[i, j] = piv[i, j] * d
            for i in range(j + 1, PANEL):
                for m in range(j + 1, i + 1):
                    piv[i, m] = piv[i, m] - low[i, j] * piv[m, j]
        masked = jnp.where(own, jnp.where(lane - base == sub, 1.0, 0.0), panel)
        fwd_u, fwd_w = [], []
        for i in range(PANEL):
            u = jnp.broadcast_to(panel[i : i + 1, :], full)
            w = jnp.broadcast_to(masked[i : i + 1, :], full)
            for j in range(i):
                u = u - low[i, j] * fwd_u[j]
                w = w - low[i, j] * fwd_w[j]
            fwd_u.append(u)
            fwd_w.append(w)
        back = [None] * PANEL
        for i in reversed(range(PANEL)):
            v = fwd_w[i] * inv[i]
            for j in range(i + 1, PANEL):
                v = v - low[j, i] * back[j]
            back[i] = v
        for r in range(k + 1, count):
            acc = cols[r, 0] * back[0]
            for j in range(1, PANEL):
                acc = acc + cols[r, j] * back[j]
            rows[r] = jnp.where(own, 0.0, rows[r]) - acc
        up, wp = fwd_u[0] * root[0], fwd_w[0] * root[0]
        for i in range(1, PANEL):
            up = jnp.where(sub == i, fwd_u[i] * root[i], up)
            wp = jnp.where(sub == i, fwd_w[i] * root[i], wp)
        upper.append(jnp.where(lane - base >= sub, up, 0.0))
        inverse.append(jnp.where(lane - base <= sub, wp, 0.0))
    return upper, inverse


def chol_kernel(g_ref, x_ref, l_ref, o_ref, a_ref, w_ref):
    n = g_ref.shape[0]
    a_ref[...] = g_ref[...]
    nb = n // BLOCK
    xs = split2(x_ref[...])
    for kb in range(nb):
        lo, hi = kb * BLOCK, (kb + 1) * BLOCK
        panels = [a_ref[lo + p * PANEL : lo + (p + 1) * PANEL, lo:hi] for p in range(BLOCK // PANEL)]
        upper, inverse = factor_block(panels)
        u = jnp.concatenate(upper, axis=0)
        w = jnp.concatenate(inverse, axis=0)
        l_ref[lo:hi, lo:hi] = u.T
        w_ref[lo:hi, lo:hi] = w
        ws = split2(w)
        if hi < n:
            l_ref[lo:hi, hi:] = jnp.zeros((BLOCK, n - hi), jnp.float32)
            below = dot3(split2(a_ref[hi:, lo:hi]), ws, NT)
            l_ref[hi:, lo:hi] = below
            bs = split2(below)
            a_ref[hi:, hi:] = a_ref[hi:, hi:] - dot3(bs, bs, NT)
        if kb:
            t = dot3(split2(l_ref[lo:hi, :lo]), split2(w_ref[:lo, :lo]), NN)
            w_ref[lo:hi, :lo] = -dot3(ws, split2(t), NN)
        if hi < n:
            w_ref[lo:hi, hi:] = jnp.zeros((BLOCK, n - hi), jnp.float32)
        wrow = split2(w_ref[lo:hi, :hi])
        xk = (xs[0][:, :hi], xs[1][:, :hi])
        o_ref[:, lo:hi] = dot3(xk, wrow, NT)


def chol_solve(gram, x):
    n = gram.shape[0]
    shape = jax.ShapeDtypeStruct((n, n), jnp.float32)
    return pl.pallas_call(
        chol_kernel,
        out_shape=(shape, jax.ShapeDtypeStruct(x.shape, jnp.float32)),
        in_specs=[pl.BlockSpec(memory_space=pltpu.VMEM)] * 2,
        out_specs=[pl.BlockSpec(memory_space=pltpu.VMEM)] * 2,
        scratch_shapes=[pltpu.VMEM((n, n), jnp.float32)] * 2,
        compiler_params=pltpu.CompilerParams(vmem_limit_bytes=32 * 1024 * 1024),
    )(gram, x)


def signs_of(value, count):
    v = lax.broadcasted_iota(jnp.int32, (count, value.shape[1]), 0) & value
    for shift in (4, 2, 1):
        v = v ^ (v >> shift)
    return (1 - 2 * (v & 1)).astype(jnp.float32)


def mix_kernel(pos_ref, x_ref, samples_ref, o_ref, h_ref):
    width = x_ref.shape[0]
    depth = x_ref.shape[1]
    sources = 32
    cols = width // sources
    hi, lo = split2(x_ref[...])
    z_bits = pos_ref[0]
    scale = 1.0 / 512.0
    for c in range(samples_ref.shape[1] // CHUNK):
        s = samples_ref[:, c * CHUNK : (c + 1) * CHUNK]
        within = s & (depth - 1)
        device = s // depth
        low = signs_of(within & 15, 16)
        high = signs_of(within // 16, depth // 16)
        for r in range(depth // 16):
            h_ref[r * 16 : (r + 1) * 16, :] = (low * high[r : r + 1, :]).astype(jnp.bfloat16)
        plane_sign = signs_of((device & 15) | ((device // 256) * 16), sources)
        zv = (device // 16) & z_bits
        zv = zv ^ (zv >> 2)
        zv = zv ^ (zv >> 1)
        z_sign = (1 - 2 * (zv & 1)).astype(jnp.float32) * scale
        h = h_ref[...]
        t = jnp.dot(hi, h, preferred_element_type=jnp.float32)
        t = t + jnp.dot(lo, h, preferred_element_type=jnp.float32)
        acc = t[:cols, :]
        for p in range(1, sources):
            acc = acc + t[p * cols : (p + 1) * cols, :] * plane_sign[p : p + 1, :]
        acc = acc * z_sign
        for b in range(CHUNK // BLOCK):
            o_ref[c * (CHUNK // BLOCK) + b] = acc[:, b * BLOCK : (b + 1) * BLOCK]


def sample_columns(columns, samples, z_index):
    width = columns.shape[0]
    count = samples.shape[0]
    return pl.pallas_call(
        mix_kernel,
        out_shape=jax.ShapeDtypeStruct((count // BLOCK, width // 32, BLOCK), jnp.float32),
        in_specs=[
            pl.BlockSpec(memory_space=pltpu.SMEM),
            pl.BlockSpec(memory_space=pltpu.VMEM),
            pl.BlockSpec(memory_space=pltpu.VMEM),
        ],
        out_specs=pl.BlockSpec(memory_space=pltpu.VMEM),
        scratch_shapes=[pltpu.VMEM((columns.shape[1], CHUNK), jnp.bfloat16)],
        compiler_params=pltpu.CompilerParams(vmem_limit_bytes=32 * 1024 * 1024),
    )(z_index.reshape(1), columns, samples.reshape(1, count))


def exchange(block, axes):
    return lax.all_to_all(block, axes, 0, 0, tiled=True)


def gather(block, axes):
    count = lax.axis_size(axes)
    return exchange(jnp.broadcast_to(block[None], (count,) + block.shape), axes)


def body(matrix, signs, samples):
    n = matrix.shape[1]
    plane = lax.axis_size(PLANE)
    depth = lax.axis_size("z")
    cols = n // plane
    z_index = lax.axis_index("z")
    signed = (signs.astype(jnp.float32)[:, None] * matrix).T
    columns = exchange(signed.reshape(plane, cols, -1), PLANE)
    partial = sample_columns(columns.reshape(n, -1), samples, z_index)
    mine = jnp.sum(exchange(partial, "z"), axis=0)
    every = gather(mine, PLANE).reshape(n, -1)
    rows = lax.dot_general(mine, every, (NT, ((), ())), precision=lax.Precision.HIGHEST)
    rows = rows.reshape(depth, cols // depth, n)
    row = jnp.sum(exchange(rows, "z"), axis=0) / jnp.float32(samples.shape[0])
    rows = gather(row, "z").reshape(cols, n)
    gram = gather(rows, PLANE).reshape(n, n)
    return chol_solve(gram, matrix)


def solution(mesh):
    fine = Mesh(mesh.devices.reshape(2, 16, 2, 4, 2), ROW_AXES)
    in_specs = (P(ROW_AXES, None), P(ROW_AXES), P())
    out_specs = (P(), P(ROW_AXES, None))
    return jax.shard_map(body, mesh=fine, in_specs=in_specs, out_specs=out_specs, check_vma=False)
```

```python
import jax
import jax.numpy as jnp
from jax import lax
from jax.experimental import pallas as pl
from jax.experimental.pallas import tpu as pltpu
from jax.sharding import Mesh
from jax.sharding import PartitionSpec as P

BLOCK = 128
CHUNK = 512
ROW_AXES = ("x_hi", "z_hi", "z_lo", "x_lo", "y", "core")
PLANE = ("x_hi", "x_lo", "y", "core")
LOWER = ((0, 0), (1, 0), (1, 1), (2, 0), (2, 1), (2, 2), (3, 0), (3, 1), (3, 2), (3, 3))
VMEM = pl.BlockSpec(memory_space=pltpu.VMEM)
SMEM = pl.BlockSpec(memory_space=pltpu.SMEM)
PARAMS = pltpu.CompilerParams(vmem_limit_bytes=32 * 1024 * 1024)


def split2(x):
    hi = x.astype(jnp.bfloat16)
    return hi, (x - hi.astype(jnp.float32)).astype(jnp.bfloat16)


def left(x):
    hi, lo = split2(x)
    return jnp.concatenate([hi, hi, lo], axis=1)


def right(x):
    hi, lo = split2(x)
    return jnp.concatenate([hi, lo, hi], axis=1)


def dot_t(a, b):
    return lax.dot_general(a, b, (((1,), (1,)), ((), ())), preferred_element_type=jnp.float32)


def factor_block(rows, c_ref):
    lane = lax.broadcasted_iota(jnp.int32, (8, BLOCK), 1)
    sub = lax.broadcasted_iota(jnp.int32, (8, BLOCK), 0)
    rows = list(rows)
    groups = len(rows)
    full = (8, BLOCK)
    upper, packed = [], []
    for k in range(groups):
        base = k * 8
        own = (lane >= base) & (lane < base + 8)
        panel = rows[k]
        col = [jnp.broadcast_to(panel[:, base + j : base + j + 1], full) for j in range(8)]
        for j in range(8):
            c_ref[k % 2, j] = col[j]
        c_ref[k % 2, 8] = panel
        spread = lambda j, i: jnp.broadcast_to(c_ref[k % 2, j, i : i + 1, :], full)
        piv = {(i, j): spread(j, i) for i in range(8) for j in range(i + 1)}
        root, inv, low, ratio = {}, {}, {}, {}
        for j in range(0, 8, 2):
            x, y, z = piv[j, j], piv[j + 1, j], piv[j + 1, j + 1]
            det = x * z - y * y
            rest = range(j + 2, 8)
            num = {}
            for i in rest:
                p, q = piv[i, j], piv[i, j + 1]
                num[i] = (p * z - q * y, q * x - p * y)
            rd = 1.0 / det
            for i in rest:
                low[i, j], low[i, j + 1] = num[i][0] * rd, num[i][1] * rd
                for m in range(j + 2, i + 1):
                    piv[i, m] = piv[i, m] - (num[i][0] * piv[m, j] + num[i][1] * piv[m, j + 1]) * rd
            inv[j] = (z * rd, y * rd, x * rd)
            root[j] = lax.rsqrt(x)
            root[j + 1] = lax.rsqrt(det) * (x * root[j])
            ratio[j] = y * (root[j] * root[j])
        fwd = []
        for i in range(8):
            w = jnp.where(own, jnp.where(lane == base + i, 1.0, 0.0), spread(8, i))
            for j in range(i - i % 2):
                w = w - low[i, j] * fwd[j]
            fwd.append(w)
        back = [None] * 8
        for i in reversed(range(0, 8, 2)):
            f, g = fwd[i], fwd[i + 1]
            x, y, z = inv[i]
            v, w = f * x - g * y, g * z - f * y
            for j in range(i + 2, 8):
                v = v - low[j, i] * back[j]
                w = w - low[j, i + 1] * back[j]
            back[i], back[i + 1] = v, w
        for r in range(k + 1, groups):
            terms = [jnp.broadcast_to(rows[r][:, base + j : base + j + 1], full) * back[j] for j in range(8)]
            while len(terms) > 1:
                terms = [x + y for x, y in zip(terms[::2], terms[1::2])]
            rows[r] = jnp.where(own, 0.0, rows[r]) - terms[0]
        up = pk = jnp.zeros(full, jnp.float32)
        for g in range(8):
            h = g - g % 2
            w = (fwd[g] if g == h else fwd[g] - ratio[h] * fwd[h]) * root[g]
            u = w
            for j in range(g, 8):
                e = piv[j, g] if g == h else piv[j, g] - ratio[h] * piv[j, h]
                u = jnp.where(lane == base + j, e * root[g], u)
            up = jnp.where(sub == g, u, up)
            pk = jnp.where(sub == g, w, pk)
        upper.append(jnp.where(lane >= base + sub, up, 0.0))
        packed.append(pk)
    inverse = [jnp.where(lane <= k * 8 + sub, packed[k], 0.0) for k in range(groups)]
    return upper, inverse


def chol_kernel(g_ref, x_ref, l_ref, o_ref, a_ref, c_ref):
    n = x_ref.shape[1]
    nb = n // BLOCK
    at = [slice(k * BLOCK, (k + 1) * BLOCK) for k in range(nb)]
    r = lax.broadcasted_iota(jnp.int32, (BLOCK, BLOCK), 0)
    c = lax.broadcasted_iota(jnp.int32, (BLOCK, BLOCK), 1)
    row_scale, col_scale, row_root = [], [], []
    for k in range(nb):
        for i in range(k, nb):
            a_ref[at[i], at[k]] = lower_block(g_ref, i, k)
        diag = jnp.where(r == c, a_ref[at[k], at[k]], 0.0)
        by_row = jnp.broadcast_to(jnp.sum(diag, axis=1, keepdims=True), (BLOCK, BLOCK))
        s = lax.rsqrt(by_row)
        row_scale.append(s)
        row_root.append(by_row * s)
        col_scale.append(lax.rsqrt(jnp.sum(diag, axis=0, keepdims=True)))
    for k in range(nb):
        for i in range(k, nb):
            a_ref[at[i], at[k]] = a_ref[at[i], at[k]] * row_scale[i] * col_scale[k]
        o_ref[:, at[k]] = x_ref[:, at[k]] * col_scale[k]
    for k in range(nb):
        panels = [a_ref[k * BLOCK + p * 8 : k * BLOCK + (p + 1) * 8, at[k]] for p in range(BLOCK // 8)]
        upper, inverse = factor_block(panels, c_ref)
        ws = right(jnp.concatenate(inverse, axis=0))
        below = {}
        for i in range(k + 1, nb):
            below[i] = dot_t(left(a_ref[at[i], at[k]]), ws)
            for j in range(k + 1, i + 1):
                a_ref[at[i], at[j]] = a_ref[at[i], at[j]] - dot_t(left(below[i]), right(below[j]))
        l_ref[at[k], at[k]] = jnp.concatenate(upper, axis=0).T * row_root[k]
        solved = dot_t(left(o_ref[:, at[k]]), ws)
        o_ref[:, at[k]] = solved
        for i in range(k + 1, nb):
            l_ref[at[i], at[k]] = below[i] * row_root[i]
            l_ref[at[k], at[i]] = jnp.zeros((BLOCK, BLOCK), jnp.float32)
            o_ref[:, at[i]] = o_ref[:, at[i]] - dot_t(left(solved), right(below[i]))


def lower_block(g_ref, i, j):
    core, slot = divmod(LOWER.index((i, j)), len(LOWER) // 2)
    parts = [g_ref[chip * 2 + core, slot * 8 : slot * 8 + 8, :] for chip in range(BLOCK // 8)]
    return jnp.concatenate(parts, axis=0)


def chol_solve(parts, x):
    n = x.shape[1]
    return pl.pallas_call(
        chol_kernel,
        out_shape=(jax.ShapeDtypeStruct((n, n), jnp.float32), jax.ShapeDtypeStruct(x.shape, jnp.float32)),
        in_specs=[VMEM, VMEM],
        out_specs=[VMEM, VMEM],
        scratch_shapes=[pltpu.VMEM((n, n), jnp.float32), pltpu.VMEM((2, 9, 8, BLOCK), jnp.float32)],
        compiler_params=PARAMS,
    )(parts, x)


def gram_kernel(place_ref, p_ref, o_ref, split_ref):
    chip, core = place_ref[0], place_ref[1]
    half = len(LOWER) // 2
    split_ref[...] = right(p_ref[...])
    for slot in range(half):
        i = jnp.where(core == 0, LOWER[slot][0], LOWER[slot + half][0])
        j = jnp.where(core == 0, LOWER[slot][1], LOWER[slot + half][1])
        rows = p_ref[pl.ds(pl.multiple_of(i * BLOCK + chip * 8, 8), 8), :]
        cols = split_ref[pl.ds(pl.multiple_of(j * BLOCK, BLOCK), BLOCK), :]
        o_ref[slot * 8 : slot * 8 + 8, :] = dot_t(left(rows), cols)


def gram_part(columns, place):
    n, depth = columns.shape
    return pl.pallas_call(
        gram_kernel,
        out_shape=jax.ShapeDtypeStruct((4 * len(LOWER), BLOCK), jnp.float32),
        in_specs=[SMEM, VMEM],
        out_specs=VMEM,
        scratch_shapes=[pltpu.VMEM((n, 3 * depth), jnp.bfloat16)],
        compiler_params=PARAMS,
    )(place, columns)


def flip_kernel(x_ref, signs_ref, o_ref):
    o_ref[...] = x_ref[...].T * signs_ref[...].astype(jnp.float32)


def signed_columns(matrix, signs):
    return pl.pallas_call(
        flip_kernel,
        out_shape=jax.ShapeDtypeStruct(matrix.shape[::-1], jnp.float32),
        in_specs=[VMEM, VMEM],
        out_specs=VMEM,
        compiler_params=PARAMS,
    )(matrix, signs.reshape(1, -1))


def signs_of(value, count):
    v = lax.broadcasted_iota(jnp.int32, (count, value.shape[1]), 0) & value
    for shift in (4, 2, 1):
        v = v ^ (v >> shift)
    return (1 - 2 * (v & 1)).astype(jnp.float32)


def mix_kernel(pos_ref, x_ref, samples_ref, o_ref, h_ref):
    width = x_ref.shape[0]
    depth = x_ref.shape[1]
    sources = 32
    cols = width // sources
    hi, lo = split2(x_ref[...])
    z_bits = pos_ref[0]
    scale = 1.0 / 512.0
    for c in range(samples_ref.shape[1] // CHUNK):
        s = samples_ref[:, c * CHUNK : (c + 1) * CHUNK]
        within = s & (depth - 1)
        device = s // depth
        low = signs_of(within & 15, 16)
        high = signs_of(within // 16, depth // 16)
        for r in range(depth // 16):
            h_ref[r * 16 : (r + 1) * 16, :] = (low * high[r : r + 1, :]).astype(jnp.bfloat16)
        plane_sign = signs_of((device & 15) | ((device // 256) * 16), sources)
        zv = (device // 16) & z_bits
        zv = zv ^ (zv >> 2)
        zv = zv ^ (zv >> 1)
        z_sign = (1 - 2 * (zv & 1)).astype(jnp.float32) * scale
        h = h_ref[...]
        t = jnp.dot(hi, h, preferred_element_type=jnp.float32)
        t = t + jnp.dot(lo, h, preferred_element_type=jnp.float32)
        acc = t[:cols, :]
        for p in range(1, sources):
            acc = acc + t[p * cols : (p + 1) * cols, :] * plane_sign[p : p + 1, :]
        acc = acc * z_sign
        o_ref[c] = acc


def sample_columns(columns, samples, z_index):
    width = columns.shape[0]
    count = samples.shape[0]
    return pl.pallas_call(
        mix_kernel,
        out_shape=jax.ShapeDtypeStruct((count // CHUNK, width // 32, CHUNK), jnp.float32),
        in_specs=[SMEM, VMEM, VMEM],
        out_specs=VMEM,
        scratch_shapes=[pltpu.VMEM((columns.shape[1], CHUNK), jnp.bfloat16)],
        compiler_params=PARAMS,
    )(z_index.reshape(1), columns, samples.reshape(1, count))


def exchange(block, axes):
    return lax.all_to_all(block, axes, 0, 0, tiled=True)


def gather(block, axes):
    count = lax.axis_size(axes)
    return exchange(jnp.broadcast_to(block[None], (count,) + block.shape), axes)


def body(matrix, signs, samples):
    rows, n = matrix.shape
    plane = lax.axis_size(PLANE)
    place = lax.axis_index(PLANE)
    columns = exchange(signed_columns(matrix, signs).reshape(plane, n // plane, rows), PLANE)
    partial = sample_columns(columns.reshape(n, rows), samples, lax.axis_index(("z_hi", "z_lo")))
    mine = jnp.sum(exchange(partial, "z_lo"), axis=0)
    mine = jnp.sum(gather(mine, "z_hi"), axis=0)
    every = gather(mine, PLANE).reshape(n, -1)
    part = gram_part(every, jnp.stack([place // 2, place % 2]))
    part = jnp.sum(gather(part, "z_lo"), axis=0) / jnp.float32(samples.shape[0])
    return chol_solve(gather(part, PLANE), matrix)


def solution(mesh):
    fine = Mesh(mesh.devices.reshape(2, 4, 4, 2, 4, 2), ROW_AXES)
    in_specs = (P(ROW_AXES, None), P(ROW_AXES), P())
    out_specs = (P(), P(ROW_AXES, None))
    return jax.shard_map(body, mesh=fine, in_specs=in_specs, out_specs=out_specs, check_vma=False)
```

```python
import jax
import jax.numpy as jnp
from jax import lax
from jax.experimental import pallas as pl
from jax.experimental.pallas import tpu as pltpu
from jax.sharding import Mesh
from jax.sharding import PartitionSpec as P

BLOCK = 128
CHUNK = 512
ROW_AXES = ("x_hi", "z_hi", "z_lo", "x_lo", "y", "core")
PLANE = ("x_hi", "x_lo", "y", "core")
CHIPS = ("x_hi", "x_lo", "y")
LOWER = ((0, 0), (1, 0), (1, 1), (2, 0), (2, 1), (2, 2), (3, 0), (3, 1), (3, 2), (3, 3))
VMEM = pl.BlockSpec(memory_space=pltpu.VMEM)
SMEM = pl.BlockSpec(memory_space=pltpu.SMEM)
PARAMS = pltpu.CompilerParams(vmem_limit_bytes=32 * 1024 * 1024)
WIDE = pltpu.CompilerParams(vmem_limit_bytes=60 * 1024 * 1024)


def split2(x):
    hi = x.astype(jnp.bfloat16)
    return hi, (x - hi.astype(jnp.float32)).astype(jnp.bfloat16)


def left(x):
    hi, lo = split2(x)
    return jnp.concatenate([hi, hi, lo], axis=1)


def right(x):
    hi, lo = split2(x)
    return jnp.concatenate([hi, lo, hi], axis=1)


def dot_t(a, b):
    return lax.dot_general(a, b, (((1,), (1,)), ((), ())), preferred_element_type=jnp.float32)


def factor_block(rows, c_ref):
    lane = lax.broadcasted_iota(jnp.int32, (8, BLOCK), 1)
    sub = lax.broadcasted_iota(jnp.int32, (8, BLOCK), 0)
    rows = list(rows)
    groups = len(rows)
    full = (8, BLOCK)
    upper, packed = [], []
    for k in range(groups):
        base = k * 8
        own = (lane >= base) & (lane < base + 8)
        panel = rows[k]
        col = [jnp.broadcast_to(panel[:, base + j : base + j + 1], full) for j in range(8)]
        for j in range(8):
            c_ref[k % 2, j] = col[j]
        c_ref[k % 2, 8] = panel
        spread = lambda j, i: jnp.broadcast_to(c_ref[k % 2, j, i : i + 1, :], full)
        piv = {(i, j): spread(j, i) for i in range(8) for j in range(i + 1)}
        root, inv, low, ratio = {}, {}, {}, {}
        for j in range(0, 8, 2):
            x, y, z = piv[j, j], piv[j + 1, j], piv[j + 1, j + 1]
            det = x * z - y * y
            rest = range(j + 2, 8)
            num = {}
            for i in rest:
                p, q = piv[i, j], piv[i, j + 1]
                num[i] = (p * z - q * y, q * x - p * y)
            rd = 1.0 / det
            for i in rest:
                low[i, j], low[i, j + 1] = num[i][0] * rd, num[i][1] * rd
                for m in range(j + 2, i + 1):
                    piv[i, m] = piv[i, m] - (num[i][0] * piv[m, j] + num[i][1] * piv[m, j + 1]) * rd
            inv[j] = (z * rd, y * rd, x * rd)
            root[j] = lax.rsqrt(x)
            root[j + 1] = lax.rsqrt(det) * (x * root[j])
            ratio[j] = y * (root[j] * root[j])
        fwd = []
        for i in range(8):
            w = jnp.where(own, jnp.where(lane == base + i, 1.0, 0.0), spread(8, i))
            for j in range(i - i % 2):
                w = w - low[i, j] * fwd[j]
            fwd.append(w)
        back = [None] * 8
        for i in reversed(range(0, 8, 2)):
            f, g = fwd[i], fwd[i + 1]
            x, y, z = inv[i]
            v, w = f * x - g * y, g * z - f * y
            for j in range(i + 2, 8):
                v = v - low[j, i] * back[j]
                w = w - low[j, i + 1] * back[j]
            back[i], back[i + 1] = v, w
        for r in range(k + 1, groups):
            terms = [jnp.broadcast_to(rows[r][:, base + j : base + j + 1], full) * back[j] for j in range(8)]
            while len(terms) > 1:
                terms = [x + y for x, y in zip(terms[::2], terms[1::2])]
            rows[r] = jnp.where(own, 0.0, rows[r]) - terms[0]
        up = pk = jnp.zeros(full, jnp.float32)
        for g in range(8):
            h = g - g % 2
            w = (fwd[g] if g == h else fwd[g] - ratio[h] * fwd[h]) * root[g]
            u = w
            for j in range(g, 8):
                e = piv[j, g] if g == h else piv[j, g] - ratio[h] * piv[j, h]
                u = jnp.where(lane == base + j, e * root[g], u)
            up = jnp.where(sub == g, u, up)
            pk = jnp.where(sub == g, w, pk)
        upper.append(jnp.where(lane >= base + sub, up, 0.0))
        packed.append(pk)
    inverse = [jnp.where(lane <= k * 8 + sub, packed[k], 0.0) for k in range(groups)]
    return upper, inverse


def chol_kernel(g_ref, x_ref, l_ref, o_ref, a_ref, c_ref):
    n = x_ref.shape[1]
    nb = n // BLOCK
    at = [slice(k * BLOCK, (k + 1) * BLOCK) for k in range(nb)]
    r = lax.broadcasted_iota(jnp.int32, (BLOCK, BLOCK), 0)
    c = lax.broadcasted_iota(jnp.int32, (BLOCK, BLOCK), 1)
    row_scale, col_scale, row_root = [], [], []
    for k in range(nb):
        for i in range(k, nb):
            a_ref[at[i], at[k]] = lower_block(g_ref, i, k)
        diag = jnp.where(r == c, a_ref[at[k], at[k]], 0.0)
        by_row = jnp.broadcast_to(jnp.sum(diag, axis=1, keepdims=True), (BLOCK, BLOCK))
        s = lax.rsqrt(by_row)
        row_scale.append(s)
        row_root.append(by_row * s)
        col_scale.append(lax.rsqrt(jnp.sum(diag, axis=0, keepdims=True)))
    for k in range(nb):
        for i in range(k, nb):
            a_ref[at[i], at[k]] = a_ref[at[i], at[k]] * row_scale[i] * col_scale[k]
        o_ref[:, at[k]] = x_ref[:, at[k]] * col_scale[k]
    for k in range(nb):
        panels = [a_ref[k * BLOCK + p * 8 : k * BLOCK + (p + 1) * 8, at[k]] for p in range(BLOCK // 8)]
        upper, inverse = factor_block(panels, c_ref)
        ws = right(jnp.concatenate(inverse, axis=0))
        below = {}
        for i in range(k + 1, nb):
            below[i] = dot_t(left(a_ref[at[i], at[k]]), ws)
            for j in range(k + 1, i + 1):
                a_ref[at[i], at[j]] = a_ref[at[i], at[j]] - dot_t(left(below[i]), right(below[j]))
        l_ref[at[k], at[k]] = jnp.concatenate(upper, axis=0).T * row_root[k]
        solved = dot_t(left(o_ref[:, at[k]]), ws)
        o_ref[:, at[k]] = solved
        for i in range(k + 1, nb):
            l_ref[at[i], at[k]] = below[i] * row_root[i]
            l_ref[at[k], at[i]] = jnp.zeros((BLOCK, BLOCK), jnp.float32)
            o_ref[:, at[i]] = o_ref[:, at[i]] - dot_t(left(solved), right(below[i]))


def lower_block(g_ref, i, j):
    first = LOWER.index((i, j)) * 8
    return jnp.concatenate([g_ref[chip, first : first + 8, :] for chip in range(BLOCK // 8)], axis=0)


def chol_solve(parts, x):
    n = x.shape[1]
    return pl.pallas_call(
        chol_kernel,
        out_shape=(jax.ShapeDtypeStruct((n, n), jnp.float32), jax.ShapeDtypeStruct(x.shape, jnp.float32)),
        in_specs=[VMEM, VMEM],
        out_specs=[VMEM, VMEM],
        scratch_shapes=[pltpu.VMEM((n, n), jnp.float32), pltpu.VMEM((2, 9, 8, BLOCK), jnp.float32)],
        compiler_params=PARAMS,
    )(parts, x)


def gram_kernel(place_ref, own_ref, other_ref, o_ref, all_ref, split_ref):
    chip, core = place_ref[0], place_ref[1]
    half = own_ref.shape[0]
    for ref, place in ((own_ref, core), (other_ref, 1 - core)):
        at = pl.ds(pl.multiple_of(place * half, half), half)
        all_ref[at, :] = ref[...]
        split_ref[at, :] = right(ref[...])
    for i in range(2 * half // BLOCK):
        width = (i + 1) * BLOCK
        rows = left(all_ref[pl.ds(pl.multiple_of(i * BLOCK + chip * 8, 8), 8), :])
        product = dot_t(rows, split_ref[:width, :])
        for j in range(i + 1):
            first = LOWER.index((i, j)) * 8
            o_ref[first : first + 8, :] = product[:, j * BLOCK : (j + 1) * BLOCK]


def gram_part(own, other, place):
    half, depth = own.shape
    return pl.pallas_call(
        gram_kernel,
        out_shape=jax.ShapeDtypeStruct((8 * len(LOWER), BLOCK), jnp.float32),
        in_specs=[SMEM, VMEM, VMEM],
        out_specs=VMEM,
        scratch_shapes=[
            pltpu.VMEM((2 * half, depth), jnp.float32),
            pltpu.VMEM((2 * half, 3 * depth), jnp.bfloat16),
        ],
        compiler_params=PARAMS,
    )(place, own, other)


def flip_kernel(x_ref, signs_ref, o_ref, buf_ref, row_ref, sems):
    rows, n = buf_ref.shape
    parts = rows // BLOCK
    group = n // 32
    sign_copy = pltpu.make_async_copy(signs_ref, row_ref, sems.at[parts])
    copies = []
    for k in range(parts):
        at = pl.ds(k * BLOCK, BLOCK)
        copies.append(pltpu.make_async_copy(x_ref.at[at, :], buf_ref.at[at, :], sems.at[k]))
    copies[0].start()
    sign_copy.start()
    for copy in copies[1:]:
        copy.start()
    sign_copy.wait()
    for k in range(parts):
        copies[k].wait()
        at = slice(k * BLOCK, (k + 1) * BLOCK)
        sign = row_ref[:, at].astype(jnp.float32)
        for c in range(n // BLOCK):
            block = buf_ref[at, c * BLOCK : (c + 1) * BLOCK].T * sign
            for q in range(BLOCK // group):
                core, chip = divmod(c * (BLOCK // group) + q, 16)
                to = (2 * chip + core) * group
                o_ref[to : to + group, at] = block[q * group : (q + 1) * group, :]


def signed_columns(matrix, signs):
    rows, n = matrix.shape
    hbm = pl.BlockSpec(memory_space=pl.ANY)
    return pl.pallas_call(
        flip_kernel,
        out_shape=jax.ShapeDtypeStruct((n, rows), jnp.float32),
        in_specs=[hbm, hbm],
        out_specs=VMEM,
        scratch_shapes=[
            pltpu.VMEM((rows, n), jnp.float32),
            pltpu.VMEM((1, rows), jnp.int32),
            pltpu.SemaphoreType.DMA((rows // BLOCK + 1,)),
        ],
        compiler_params=WIDE,
    )(matrix, signs.reshape(1, -1))


def signs_of(value, count):
    v = lax.broadcasted_iota(jnp.int32, (count, value.shape[1]), 0) & value
    for shift in (4, 2, 1):
        v = v ^ (v >> shift)
    return (1 - 2 * (v & 1)).astype(jnp.float32)


def mix_kernel(pos_ref, x_ref, samples_ref, o_ref, h_ref):
    width = x_ref.shape[0]
    depth = x_ref.shape[1]
    sources = 32
    cols = width // sources
    hi, lo = split2(x_ref[...])
    z_bits = pos_ref[0]
    scale = 1.0 / 512.0
    for c in range(samples_ref.shape[1] // CHUNK):
        s = samples_ref[:, c * CHUNK : (c + 1) * CHUNK]
        within = s & (depth - 1)
        device = s // depth
        low = signs_of(within & 15, 16)
        high = signs_of(within // 16, depth // 16)
        for r in range(depth // 16):
            h_ref[r * 16 : (r + 1) * 16, :] = (low * high[r : r + 1, :]).astype(jnp.bfloat16)
        plane_sign = signs_of((device & 15) | ((device // 256) * 16), sources)
        zv = (device // 16) & z_bits
        zv = zv ^ (zv >> 2)
        zv = zv ^ (zv >> 1)
        z_sign = (1 - 2 * (zv & 1)).astype(jnp.float32) * scale
        h = h_ref[...]
        t = jnp.dot(hi, h, preferred_element_type=jnp.float32)
        t = t + jnp.dot(lo, h, preferred_element_type=jnp.float32)
        acc = t[:cols, :]
        for p in range(1, sources):
            acc = acc + t[p * cols : (p + 1) * cols, :] * plane_sign[p : p + 1, :]
        acc = acc * z_sign
        o_ref[c] = acc


def sample_columns(columns, samples, z_index):
    width = columns.shape[0]
    count = samples.shape[0]
    return pl.pallas_call(
        mix_kernel,
        out_shape=jax.ShapeDtypeStruct((count // CHUNK, width // 32, CHUNK), jnp.float32),
        in_specs=[SMEM, VMEM, VMEM],
        out_specs=VMEM,
        scratch_shapes=[pltpu.VMEM((columns.shape[1], CHUNK), jnp.bfloat16)],
        compiler_params=PARAMS,
    )(z_index.reshape(1), columns, samples.reshape(1, count))


def exchange(block, axes):
    return lax.all_to_all(block, axes, 0, 0, tiled=True)


def gather(block, axes):
    count = lax.axis_size(axes)
    return exchange(jnp.broadcast_to(block[None], (count,) + block.shape), axes)


def body(matrix, signs, samples):
    rows, n = matrix.shape
    plane = lax.axis_size(PLANE)
    columns = exchange(signed_columns(matrix, signs).reshape(plane, n // plane, rows), PLANE)
    partial = sample_columns(columns.reshape(n, rows), samples, lax.axis_index(("z_hi", "z_lo")))
    mine = jnp.sum(exchange(partial, "z_lo"), axis=0)
    mine = jnp.sum(gather(mine, "z_hi"), axis=0)
    own = gather(mine, CHIPS).reshape(n // 2, -1)
    other = lax.ppermute(own, "core", [(0, 1), (1, 0)])
    part = gram_part(own, other, jnp.stack([lax.axis_index(CHIPS), lax.axis_index("core")]))
    part = jnp.sum(gather(part, "z_lo"), axis=0) / jnp.float32(samples.shape[0])
    return chol_solve(gather(part, CHIPS), matrix)


def solution(mesh):
    fine = Mesh(mesh.devices.reshape(2, 4, 4, 2, 4, 2), ROW_AXES)
    in_specs = (P(ROW_AXES, None), P(ROW_AXES), P())
    out_specs = (P(), P(ROW_AXES, None))
    return jax.shard_map(body, mesh=fine, in_specs=in_specs, out_specs=out_specs, check_vma=False)
```

```python
import jax
import jax.numpy as jnp
from jax import lax
from jax.experimental import pallas as pl
from jax.experimental.pallas import tpu as pltpu
from jax.sharding import Mesh
from jax.sharding import PartitionSpec as P

BLOCK = 128
CHUNK = 512
SHARE = 256
ROW_AXES = ("x_hi", "z_hi", "z_lo", "x_lo", "y", "core")
PLANE = ("x_hi", "x_lo", "y", "core")
CHIPS = ("x_hi", "x_lo", "y")
NEAR = ("z_lo", "core")
LOWER = ((0, 0), (1, 0), (1, 1), (2, 0), (2, 1), (2, 2), (3, 0), (3, 1), (3, 2), (3, 3))
VMEM = pl.BlockSpec(memory_space=pltpu.VMEM)
SMEM = pl.BlockSpec(memory_space=pltpu.SMEM)
PARAMS = pltpu.CompilerParams(vmem_limit_bytes=32 * 1024 * 1024)
WIDE = pltpu.CompilerParams(vmem_limit_bytes=60 * 1024 * 1024)


def split2(x):
    hi = x.astype(jnp.bfloat16)
    return hi, (x - hi.astype(jnp.float32)).astype(jnp.bfloat16)


def left(x):
    hi, lo = split2(x)
    return jnp.concatenate([hi, hi, lo], axis=1)


def right(x):
    hi, lo = split2(x)
    return jnp.concatenate([hi, lo, hi], axis=1)


def dot_t(a, b):
    return lax.dot_general(a, b, (((1,), (1,)), ((), ())), preferred_element_type=jnp.float32)


def factor_block(rows, c_ref, u_ref, w_ref):
    lane = lax.broadcasted_iota(jnp.int32, (8, BLOCK), 1)
    sub = lax.broadcasted_iota(jnp.int32, (8, BLOCK), 0)
    rows = list(rows)
    groups = len(rows)
    full = (8, BLOCK)
    for k in range(groups):
        base = k * 8
        own = (lane >= base) & (lane < base + 8)
        panel = rows[k]
        for j in range(8):
            c_ref[k % 2, j] = jnp.broadcast_to(panel[:, base + j : base + j + 1], full)
        c_ref[k % 2, 8] = panel
        spread = lambda j, i: jnp.broadcast_to(c_ref[k % 2, j, i : i + 1, :], full)
        piv = {(i, j): spread(j, i) for i in range(8) for j in range(i + 1)}
        root, inv, low, ratio = {}, {}, {}, {}
        for j in range(0, 8, 2):
            x, y, z = piv[j, j], piv[j + 1, j], piv[j + 1, j + 1]
            det = x * z - y * y
            rd = 1.0 / det
            for i in range(j + 2, 8):
                p, q = piv[i, j], piv[i, j + 1]
                f, g = p * z - q * y, q * x - p * y
                low[i, j], low[i, j + 1] = f * rd, g * rd
                for m in range(j + 2, i + 1):
                    if i < j + 4:
                        piv[i, m] = piv[i, m] - (f * piv[m, j] + g * piv[m, j + 1]) * rd
                    else:
                        piv[i, m] = piv[i, m] - low[i, j] * piv[m, j] - low[i, j + 1] * piv[m, j + 1]
            inv[j] = (z * rd, y * rd, x * rd)
            root[j] = lax.rsqrt(x)
            root[j + 1] = lax.rsqrt(det) * (x * root[j])
            ratio[j] = y * (root[j] * root[j])
        fwd, fwd_u = [], []
        for i in range(8):
            u = spread(8, i)
            w = jnp.where(own, jnp.where(lane == base + i, 1.0, 0.0), u)
            for j in range(i - i % 2):
                w = w - low[i, j] * fwd[j]
                u = u - low[i, j] * fwd_u[j]
            fwd.append(w)
            fwd_u.append(u)
        back = [None] * 8
        for i in reversed(range(0, 8, 2)):
            f, g = fwd[i], fwd[i + 1]
            x, y, z = inv[i]
            v, w = f * x - g * y, g * z - f * y
            for j in range(i + 2, 8):
                v = v - low[j, i] * back[j]
                w = w - low[j, i + 1] * back[j]
            back[i], back[i + 1] = v, w
        for r in range(k + 1, groups):
            terms = [jnp.broadcast_to(rows[r][:, base + j : base + j + 1], full) * back[j] for j in range(8)]
            while len(terms) > 1:
                terms = [x + y for x, y in zip(terms[::2], terms[1::2])]
            rows[r] = jnp.where(own, 0.0, rows[r]) - terms[0]
        for g in range(8):
            h = g - g % 2
            w = fwd[g] if g == h else fwd[g] - ratio[h] * fwd[h]
            u = fwd_u[g] if g == h else fwd_u[g] - ratio[h] * fwd_u[h]
            u_ref[base + g : base + g + 1, :] = jnp.where(lane >= base + g, u * root[g], 0.0)[:1, :]
            w_ref[base + g : base + g + 1, :] = jnp.where(lane <= base + g, w * root[g], 0.0)[:1, :]


def chol_kernel(g_ref, x_ref, l_out, o_out, a_ref, l_ref, o_ref, c_ref, u_ref, w_ref, sems):
    n = x_ref.shape[1]
    nb = n // BLOCK
    at = [slice(k * BLOCK, (k + 1) * BLOCK) for k in range(nb)]
    r = lax.broadcasted_iota(jnp.int32, (BLOCK, BLOCK), 0)
    c = lax.broadcasted_iota(jnp.int32, (BLOCK, BLOCK), 1)
    row_scale, col_scale, row_root = [], [], []
    copies = []
    for k in range(nb):
        diag = jnp.where(r == c, lower_block(g_ref, k, k), 0.0)
        by_row = jnp.broadcast_to(jnp.sum(diag, axis=1, keepdims=True), (BLOCK, BLOCK))
        s = lax.rsqrt(by_row)
        row_scale.append(s)
        row_root.append(by_row * s)
        col_scale.append(lax.rsqrt(jnp.sum(diag, axis=0, keepdims=True)))
    for k in range(nb):
        for i in range(k, nb):
            a_ref[at[i], at[k]] = lower_block(g_ref, i, k) * row_scale[i] * col_scale[k]
    for k in range(nb):
        panels = [a_ref[k * BLOCK + p * 8 : k * BLOCK + (p + 1) * 8, at[k]] for p in range(BLOCK // 8)]
        factor_block(panels, c_ref, u_ref.at[k % 2], w_ref.at[k % 2])
        ws = right(w_ref[k % 2])
        below = {}
        for i in range(k + 1, nb):
            below[i] = dot_t(left(a_ref[at[i], at[k]]), ws)
            for j in range(k + 1, i + 1):
                a_ref[at[i], at[j]] = a_ref[at[i], at[j]] - dot_t(left(below[i]), right(below[j]))
        before = x_ref[:, at[k]] * col_scale[k]
        if k:
            before = before - o_ref[:, at[k]]
        solved = dot_t(left(before), ws)
        o_ref[:, at[k]] = solved
        for i in range(k + 1, nb):
            add = dot_t(left(solved), right(below[i]))
            o_ref[:, at[i]] = o_ref[:, at[i]] + add if k else add
        for i in range(k):
            l_ref[at[i], at[k]] = jnp.zeros((BLOCK, BLOCK), jnp.float32)
        l_ref[at[k], at[k]] = u_ref[k % 2].T * row_root[k]
        for i in range(k + 1, nb):
            l_ref[at[i], at[k]] = below[i] * row_root[i]
        copies.append(pltpu.make_async_copy(o_ref.at[:, at[k]], o_out.at[:, at[k]], sems.at[2 * k]))
        copies.append(pltpu.make_async_copy(l_ref.at[:, at[k]], l_out.at[:, at[k]], sems.at[2 * k + 1]))
        copies[-2].start()
        copies[-1].start()
    for copy in copies:
        copy.wait()


def lower_block(g_ref, i, j):
    first = LOWER.index((i, j)) * 8
    return jnp.concatenate([g_ref[chip, first : first + 8, :] for chip in range(BLOCK // 8)], axis=0)


def chol_solve(parts, x):
    rows, n = x.shape
    return pl.pallas_call(
        chol_kernel,
        out_shape=(jax.ShapeDtypeStruct((n, n), jnp.float32), jax.ShapeDtypeStruct(x.shape, jnp.float32)),
        in_specs=[VMEM, VMEM],
        out_specs=[pl.BlockSpec(memory_space=pl.ANY)] * 2,
        scratch_shapes=[
            pltpu.VMEM((n, n), jnp.float32),
            pltpu.VMEM((n, n), jnp.float32),
            pltpu.VMEM((rows, n), jnp.float32),
            pltpu.VMEM((2, 9, 8, BLOCK), jnp.float32),
            pltpu.VMEM((2, BLOCK, BLOCK), jnp.float32),
            pltpu.VMEM((2, BLOCK, BLOCK), jnp.float32),
            pltpu.SemaphoreType.DMA((2 * (n // BLOCK),)),
        ],
        compiler_params=PARAMS,
    )(parts, x)


def gram_kernel(chip_ref, p_ref, o_ref):
    blocks = p_ref.shape[0] // BLOCK
    first = chip_ref[0] * 8
    rows = [p_ref[pl.ds(pl.multiple_of(i * BLOCK + first, 8), 8), :] for i in range(blocks)]
    product = dot_t(left(jnp.concatenate(rows, axis=0)), right(p_ref[...]))
    for t, (i, j) in enumerate(LOWER):
        o_ref[t * 8 : t * 8 + 8, :] = product[i * 8 : i * 8 + 8, j * BLOCK : (j + 1) * BLOCK]


def gram_part(columns, chip):
    return pl.pallas_call(
        gram_kernel,
        out_shape=jax.ShapeDtypeStruct((8 * len(LOWER), BLOCK), jnp.float32),
        in_specs=[SMEM, VMEM],
        out_specs=VMEM,
        compiler_params=PARAMS,
    )(chip.reshape(1), columns)


def flip_kernel(x_ref, signs_ref, o_ref, buf_ref, row_ref, sems):
    rows, n = buf_ref.shape
    parts = rows // BLOCK
    sign_copy = pltpu.make_async_copy(signs_ref, row_ref, sems.at[parts])
    copies = []
    for k in range(parts):
        at = pl.ds(k * BLOCK, BLOCK)
        copies.append(pltpu.make_async_copy(x_ref.at[at, :], buf_ref.at[at, :], sems.at[k]))
    copies[0].start()
    sign_copy.start()
    for copy in copies[1:]:
        copy.start()
    sign_copy.wait()
    for k in range(parts):
        copies[k].wait()
        at = slice(k * BLOCK, (k + 1) * BLOCK)
        sign = row_ref[:, at].astype(jnp.float32)
        for c in range(n // BLOCK):
            cols = slice(c * BLOCK, (c + 1) * BLOCK)
            o_ref[cols, at] = buf_ref[at, cols].T * sign


def signed_columns(matrix, signs):
    rows, n = matrix.shape
    hbm = pl.BlockSpec(memory_space=pl.ANY)
    return pl.pallas_call(
        flip_kernel,
        out_shape=jax.ShapeDtypeStruct((n, rows), jnp.float32),
        in_specs=[hbm, hbm],
        out_specs=VMEM,
        scratch_shapes=[
            pltpu.VMEM((rows, n), jnp.float32),
            pltpu.VMEM((1, rows), jnp.int32),
            pltpu.SemaphoreType.DMA((rows // BLOCK + 1,)),
        ],
        compiler_params=WIDE,
    )(matrix, signs.reshape(1, -1))


def signs_of(value, count):
    v = lax.broadcasted_iota(jnp.int32, (count, value.shape[1]), 0) & value
    for shift in (4, 2, 1):
        v = v ^ (v >> shift)
    return (1 - 2 * (v & 1)).astype(jnp.float32)


def mix_kernel(pos_ref, x_ref, samples_ref, o_ref, h_ref):
    width = x_ref.shape[0]
    depth = x_ref.shape[1]
    sources = 32
    cols = width // sources
    hi, lo = split2(x_ref[...])
    z_bits = pos_ref[0]
    scale = 1.0 / 512.0
    for c in range(samples_ref.shape[1] // CHUNK):
        s = samples_ref[:, c * CHUNK : (c + 1) * CHUNK]
        within = s & (depth - 1)
        device = s // depth
        low = signs_of(within & 15, 16)
        high = signs_of(within // 16, depth // 16)
        for r in range(depth // 16):
            h_ref[r * 16 : (r + 1) * 16, :] = (low * high[r : r + 1, :]).astype(jnp.bfloat16)
        plane_sign = signs_of((device & 15) | ((device // 256) * 16), sources)
        zv = (device // 16) & z_bits
        zv = zv ^ (zv >> 2)
        zv = zv ^ (zv >> 1)
        z_sign = (1 - 2 * (zv & 1)).astype(jnp.float32) * scale
        h = h_ref[...]
        t = jnp.dot(hi, h, preferred_element_type=jnp.float32)
        t = t + jnp.dot(lo, h, preferred_element_type=jnp.float32)
        acc = t[:cols, :]
        for p in range(1, sources):
            acc = acc + t[p * cols : (p + 1) * cols, :] * plane_sign[p : p + 1, :]
        acc = acc * z_sign
        for b in range(CHUNK // SHARE):
            o_ref[c * (CHUNK // SHARE) + b] = acc[:, b * SHARE : (b + 1) * SHARE]


def sample_columns(columns, samples, z_index):
    width = columns.shape[0]
    count = samples.shape[0]
    return pl.pallas_call(
        mix_kernel,
        out_shape=jax.ShapeDtypeStruct((count // SHARE, width // 32, SHARE), jnp.float32),
        in_specs=[SMEM, VMEM, VMEM],
        out_specs=VMEM,
        scratch_shapes=[pltpu.VMEM((columns.shape[1], CHUNK), jnp.bfloat16)],
        compiler_params=PARAMS,
    )(z_index.reshape(1), columns, samples.reshape(1, count))


def exchange(block, axes):
    return lax.all_to_all(block, axes, 0, 0, tiled=True)


def gather(block, axes):
    count = lax.axis_size(axes)
    return exchange(jnp.broadcast_to(block[None], (count,) + block.shape), axes)


def body(matrix, signs, samples):
    rows, n = matrix.shape
    plane = lax.axis_size(PLANE)
    columns = exchange(signed_columns(matrix, signs).reshape(plane, n // plane, rows), PLANE)
    partial = sample_columns(columns.reshape(n, rows), samples, lax.axis_index(("z_hi", "z_lo")))
    mine = exchange(partial, NEAR).reshape(lax.axis_size("z_lo"), 2 * (n // plane), -1)
    mine = jnp.sum(gather(jnp.sum(mine, axis=0), "z_hi"), axis=0)
    every = gather(mine, CHIPS).reshape(n, -1)
    part = gram_part(every, lax.axis_index(CHIPS))
    part = jnp.sum(gather(part, NEAR), axis=0) / jnp.float32(samples.shape[0])
    return chol_solve(gather(part, CHIPS), matrix)


def solution(mesh):
    fine = Mesh(mesh.devices.reshape(2, 4, 4, 2, 4, 2), ROW_AXES)
    in_specs = (P(ROW_AXES, None), P(ROW_AXES), P())
    out_specs = (P(), P(ROW_AXES, None))
    return jax.shard_map(body, mesh=fine, in_specs=in_specs, out_specs=out_specs, check_vma=False)
```

```python
import jax
import jax.numpy as jnp
from jax import lax
from jax.experimental import pallas as pl
from jax.experimental.pallas import tpu as pltpu
from jax.sharding import Mesh
from jax.sharding import PartitionSpec as P

BLOCK = 128
CHUNK = 512
SHARE = 256
ROW_AXES = ("x_hi", "z_hi", "z_lo", "x_lo", "y", "core")
CHIPS = ("x_hi", "x_lo", "y")
NEAR = ("z_lo", "core")
LOWER = ((0, 0), (1, 0), (1, 1), (2, 0), (2, 1), (2, 2), (3, 0), (3, 1), (3, 2), (3, 3))
VMEM = pl.BlockSpec(memory_space=pltpu.VMEM)
SMEM = pl.BlockSpec(memory_space=pltpu.SMEM)
PARAMS = pltpu.CompilerParams(vmem_limit_bytes=32 * 1024 * 1024)
WIDE = pltpu.CompilerParams(vmem_limit_bytes=60 * 1024 * 1024)


def split2(x):
    hi = x.astype(jnp.bfloat16)
    return hi, (x - hi.astype(jnp.float32)).astype(jnp.bfloat16)


def left(x):
    hi, lo = split2(x)
    return jnp.concatenate([hi, hi, lo], axis=1)


def right(x):
    hi, lo = split2(x)
    return jnp.concatenate([hi, lo, hi], axis=1)


def dot_t(a, b):
    return lax.dot_general(a, b, (((1,), (1,)), ((), ())), preferred_element_type=jnp.float32)


def factor_block(rows, c_ref, u_ref, w_ref):
    lane = lax.broadcasted_iota(jnp.int32, (8, BLOCK), 1)
    sub = lax.broadcasted_iota(jnp.int32, (8, BLOCK), 0)
    rows = list(rows)
    groups = len(rows)
    full = (8, BLOCK)
    for k in range(groups):
        base = k * 8
        own = (lane >= base) & (lane < base + 8)
        panel = rows[k]
        for j in range(8):
            c_ref[k % 2, j] = jnp.broadcast_to(panel[:, base + j : base + j + 1], full)
        c_ref[k % 2, 8] = panel
        spread = lambda j, i: jnp.broadcast_to(c_ref[k % 2, j, i : i + 1, :], full)
        piv = {(i, j): spread(j, i) for i in range(8) for j in range(i + 1)}
        root, inv, low, ratio = {}, {}, {}, {}
        for j in range(0, 8, 2):
            x, y, z = piv[j, j], piv[j + 1, j], piv[j + 1, j + 1]
            det = x * z - y * y
            rd = 1.0 / det
            for i in range(j + 2, 8):
                p, q = piv[i, j], piv[i, j + 1]
                f, g = p * z - q * y, q * x - p * y
                low[i, j], low[i, j + 1] = f * rd, g * rd
                for m in range(j + 2, i + 1):
                    if i < j + 4:
                        piv[i, m] = piv[i, m] - (f * piv[m, j] + g * piv[m, j + 1]) * rd
                    else:
                        piv[i, m] = piv[i, m] - low[i, j] * piv[m, j] - low[i, j + 1] * piv[m, j + 1]
            inv[j] = (z * rd, y * rd, x * rd)
            root[j] = lax.rsqrt(x)
            root[j + 1] = lax.rsqrt(det) * (x * root[j])
            ratio[j] = y * (root[j] * root[j])
        fwd, fwd_u = [], []
        for i in range(8):
            u = spread(8, i)
            w = jnp.where(own, jnp.where(lane == base + i, 1.0, 0.0), u)
            for j in range(i - i % 2):
                w = w - low[i, j] * fwd[j]
                u = u - low[i, j] * fwd_u[j]
            fwd.append(w)
            fwd_u.append(u)
        back = [None] * 8
        for i in reversed(range(0, 8, 2)):
            f, g = fwd[i], fwd[i + 1]
            x, y, z = inv[i]
            v, w = f * x - g * y, g * z - f * y
            for j in range(i + 2, 8):
                v = v - low[j, i] * back[j]
                w = w - low[j, i + 1] * back[j]
            back[i], back[i + 1] = v, w
        for r in range(k + 1, groups):
            terms = [jnp.broadcast_to(rows[r][:, base + j : base + j + 1], full) * back[j] for j in range(8)]
            while len(terms) > 1:
                terms = [x + y for x, y in zip(terms[::2], terms[1::2])]
            rows[r] = jnp.where(own, 0.0, rows[r]) - terms[0]
        for g in range(8):
            h = g - g % 2
            w = fwd[g] if g == h else fwd[g] - ratio[h] * fwd[h]
            u = fwd_u[g] if g == h else fwd_u[g] - ratio[h] * fwd_u[h]
            u_ref[base + g : base + g + 1, :] = jnp.where(lane >= base + g, u * root[g], 0.0)[:1, :]
            w_ref[base + g : base + g + 1, :] = jnp.where(lane <= base + g, w * root[g], 0.0)[:1, :]


def chol_kernel(core_ref, own_ref, other_ref, x_ref, l_out, o_out, a_ref, l_ref, o_ref, c_ref, u_ref, w_ref, sems):
    n = x_ref.shape[1]
    nb = n // BLOCK
    at = [slice(k * BLOCK, (k + 1) * BLOCK) for k in range(nb)]
    r = lax.broadcasted_iota(jnp.int32, (BLOCK, BLOCK), 0)
    c = lax.broadcasted_iota(jnp.int32, (BLOCK, BLOCK), 1)
    row_scale, col_scale, row_root = [], [], []
    copies = []
    gram = lambda i, j: lower_block(core_ref[0], own_ref, other_ref, i, j)
    for k in range(nb):
        diag = jnp.where(r == c, gram(k, k), 0.0)
        by_row = jnp.broadcast_to(jnp.sum(diag, axis=1, keepdims=True), (BLOCK, BLOCK))
        s = lax.rsqrt(by_row)
        row_scale.append(s)
        row_root.append(by_row * s)
        col_scale.append(lax.rsqrt(jnp.sum(diag, axis=0, keepdims=True)))
    for k in range(nb):
        for i in range(k, nb):
            a_ref[at[i], at[k]] = gram(i, k) * row_scale[i] * col_scale[k]
    for k in range(nb):
        panels = [a_ref[k * BLOCK + p * 8 : k * BLOCK + (p + 1) * 8, at[k]] for p in range(BLOCK // 8)]
        factor_block(panels, c_ref, u_ref.at[k % 2], w_ref.at[k % 2])
        ws = right(w_ref[k % 2])
        below = {}
        for i in range(k + 1, nb):
            below[i] = dot_t(left(a_ref[at[i], at[k]]), ws)
            for j in range(k + 1, i + 1):
                a_ref[at[i], at[j]] = a_ref[at[i], at[j]] - dot_t(left(below[i]), right(below[j]))
        before = x_ref[:, at[k]] * col_scale[k]
        if k:
            before = before - o_ref[:, at[k]]
        solved = dot_t(left(before), ws)
        o_ref[:, at[k]] = solved
        for i in range(k + 1, nb):
            add = dot_t(left(solved), right(below[i]))
            o_ref[:, at[i]] = o_ref[:, at[i]] + add if k else add
        for i in range(k):
            l_ref[at[i], at[k]] = jnp.zeros((BLOCK, BLOCK), jnp.float32)
        l_ref[at[k], at[k]] = u_ref[k % 2].T * row_root[k]
        for i in range(k + 1, nb):
            l_ref[at[i], at[k]] = below[i] * row_root[i]
        copies.append(pltpu.make_async_copy(o_ref.at[:, at[k]], o_out.at[:, at[k]], sems.at[2 * k]))
        copies.append(pltpu.make_async_copy(l_ref.at[:, at[k]], l_out.at[:, at[k]], sems.at[2 * k + 1]))
        copies[-2].start()
        copies[-1].start()
    for copy in copies:
        copy.wait()


def lower_block(core, own_ref, other_ref, i, j):
    half, slot = divmod(LOWER.index((i, j)), len(LOWER) // 2)
    mine = jnp.broadcast_to(core, (8, BLOCK)) == half
    at = slice(slot * 8, slot * 8 + 8)
    parts = [jnp.where(mine, own_ref[chip, at, :], other_ref[chip, at, :]) for chip in range(BLOCK // 8)]
    return jnp.concatenate(parts, axis=0)


def chol_solve(core, own, other, x):
    rows, n = x.shape
    return pl.pallas_call(
        chol_kernel,
        out_shape=(jax.ShapeDtypeStruct((n, n), jnp.float32), jax.ShapeDtypeStruct(x.shape, jnp.float32)),
        in_specs=[SMEM, VMEM, VMEM, VMEM],
        out_specs=[pl.BlockSpec(memory_space=pl.ANY)] * 2,
        scratch_shapes=[
            pltpu.VMEM((n, n), jnp.float32),
            pltpu.VMEM((n, n), jnp.float32),
            pltpu.VMEM((rows, n), jnp.float32),
            pltpu.VMEM((2, 9, 8, BLOCK), jnp.float32),
            pltpu.VMEM((2, BLOCK, BLOCK), jnp.float32),
            pltpu.VMEM((2, BLOCK, BLOCK), jnp.float32),
            pltpu.SemaphoreType.DMA((2 * (n // BLOCK),)),
        ],
        compiler_params=PARAMS,
    )(core.reshape(1), own, other, x)


def gram_kernel(chip_ref, p_ref, o_ref):
    blocks = p_ref.shape[0] // BLOCK
    first = chip_ref[0] * 8
    rows = [p_ref[pl.ds(pl.multiple_of(i * BLOCK + first, 8), 8), :] for i in range(blocks)]
    product = dot_t(left(jnp.concatenate(rows, axis=0)), right(p_ref[...]))
    for t, (i, j) in enumerate(LOWER):
        o_ref[t * 8 : t * 8 + 8, :] = product[i * 8 : i * 8 + 8, j * BLOCK : (j + 1) * BLOCK]


def gram_part(columns, chip):
    return pl.pallas_call(
        gram_kernel,
        out_shape=jax.ShapeDtypeStruct((8 * len(LOWER), BLOCK), jnp.float32),
        in_specs=[SMEM, VMEM],
        out_specs=VMEM,
        compiler_params=PARAMS,
    )(chip.reshape(1), columns)


def flip_kernel(x_ref, signs_ref, o_ref, buf_ref, row_ref, sems):
    rows, n = buf_ref.shape
    parts = rows // BLOCK
    sign_copy = pltpu.make_async_copy(signs_ref, row_ref, sems.at[parts])
    copies = []
    for k in range(parts):
        at = pl.ds(k * BLOCK, BLOCK)
        copies.append(pltpu.make_async_copy(x_ref.at[at, :], buf_ref.at[at, :], sems.at[k]))
    copies[0].start()
    sign_copy.start()
    for copy in copies[1:]:
        copy.start()
    sign_copy.wait()
    for k in range(parts):
        copies[k].wait()
        at = slice(k * BLOCK, (k + 1) * BLOCK)
        sign = row_ref[:, at].astype(jnp.float32)
        for c in range(n // BLOCK):
            cols = slice(c * BLOCK, (c + 1) * BLOCK)
            o_ref[cols, at] = buf_ref[at, cols].T * sign


def signed_columns(matrix, signs):
    rows, n = matrix.shape
    hbm = pl.BlockSpec(memory_space=pl.ANY)
    return pl.pallas_call(
        flip_kernel,
        out_shape=jax.ShapeDtypeStruct((n, rows), jnp.float32),
        in_specs=[hbm, hbm],
        out_specs=VMEM,
        scratch_shapes=[
            pltpu.VMEM((rows, n), jnp.float32),
            pltpu.VMEM((1, rows), jnp.int32),
            pltpu.SemaphoreType.DMA((rows // BLOCK + 1,)),
        ],
        compiler_params=WIDE,
    )(matrix, signs.reshape(1, -1))


def signs_of(value, count):
    v = lax.broadcasted_iota(jnp.int32, (count, value.shape[1]), 0) & value
    for shift in (4, 2, 1):
        v = v ^ (v >> shift)
    return (1 - 2 * (v & 1)).astype(jnp.float32)


def mix_kernel(place_ref, x_ref, samples_ref, o_ref, h_ref):
    width, depth = x_ref.shape
    sources = 16
    cols = width // sources
    hi, lo = split2(x_ref[...])
    mask = place_ref[0] * 16 + place_ref[1]
    scale = 1.0 / 512.0
    for c in range(samples_ref.shape[1] // CHUNK):
        s = samples_ref[:, c * CHUNK : (c + 1) * CHUNK]
        within = s & (depth - 1)
        device = s // depth
        low = signs_of(within & 15, 16)
        high = signs_of(within // 16, depth // 16)
        for r in range(depth // 16):
            h_ref[r * 16 : (r + 1) * 16, :] = (low * high[r : r + 1, :]).astype(jnp.bfloat16)
        chip_sign = signs_of(((device // 2) & 7) | ((device // 256) * 8), sources)
        v = device & mask
        for shift in (4, 2, 1):
            v = v ^ (v >> shift)
        own_sign = (1 - 2 * (v & 1)).astype(jnp.float32) * scale
        h = h_ref[...]
        t = jnp.dot(hi, h, preferred_element_type=jnp.float32)
        t = t + jnp.dot(lo, h, preferred_element_type=jnp.float32)
        acc = t[:cols, :]
        for p in range(1, sources):
            acc = acc + t[p * cols : (p + 1) * cols, :] * chip_sign[p : p + 1, :]
        acc = acc * own_sign
        for b in range(CHUNK // SHARE):
            o_ref[c * (CHUNK // SHARE) + b] = acc[:, b * SHARE : (b + 1) * SHARE]


def sample_columns(columns, samples, place):
    width = columns.shape[0]
    count = samples.shape[0]
    return pl.pallas_call(
        mix_kernel,
        out_shape=jax.ShapeDtypeStruct((count // SHARE, width // 16, SHARE), jnp.float32),
        in_specs=[SMEM, VMEM, VMEM],
        out_specs=VMEM,
        scratch_shapes=[pltpu.VMEM((columns.shape[1], CHUNK), jnp.bfloat16)],
        compiler_params=PARAMS,
    )(place, columns, samples.reshape(1, count))


def exchange(block, axes):
    return lax.all_to_all(block, axes, 0, 0, tiled=True)


def gather(block, axes):
    count = lax.axis_size(axes)
    return exchange(jnp.broadcast_to(block[None], (count,) + block.shape), axes)


def body(matrix, signs, samples):
    rows, n = matrix.shape
    chips = lax.axis_size(CHIPS)
    core = lax.axis_index("core")
    columns = exchange(signed_columns(matrix, signs).reshape(chips, n // chips, rows), CHIPS)
    place = jnp.stack([lax.axis_index(("z_hi", "z_lo")), core])
    mine = jnp.sum(exchange(sample_columns(columns.reshape(n, rows), samples, place), NEAR), axis=0)
    mine = jnp.sum(gather(mine, "z_hi"), axis=0)
    every = gather(mine, CHIPS).reshape(n, -1)
    part = gram_part(every, lax.axis_index(CHIPS)).reshape(1, 2, 4 * len(LOWER), BLOCK)
    part = jnp.broadcast_to(part, (lax.axis_size("z_lo"),) + part.shape[1:])
    part = jnp.sum(exchange(part.reshape((-1,) + part.shape[2:]), NEAR), axis=0) / jnp.float32(samples.shape[0])
    own = gather(part, CHIPS)
    other = lax.ppermute(own, "core", [(0, 1), (1, 0)])
    return chol_solve(core, own, other, matrix)


def solution(mesh):
    fine = Mesh(mesh.devices.reshape(2, 4, 4, 2, 4, 2), ROW_AXES)
    in_specs = (P(ROW_AXES, None), P(ROW_AXES), P())
    out_specs = (P(), P(ROW_AXES, None))
    return jax.shard_map(body, mesh=fine, in_specs=in_specs, out_specs=out_specs, check_vma=False)
```

```python
import jax
import jax.numpy as jnp
from jax import lax
from jax.experimental import pallas as pl
from jax.experimental.pallas import tpu as pltpu
from jax.sharding import Mesh
from jax.sharding import PartitionSpec as P

BLOCK = 128
CHUNK = 512
SHARE = 256
ROW_AXES = ("x_hi", "z_hi", "z_lo", "x_lo", "y", "core")
PLANE = ("x_hi", "x_lo", "y", "core")
CHIPS = ("x_hi", "x_lo", "y")
NEAR = ("z_lo", "core")
LOWER = ((0, 0), (1, 0), (1, 1), (2, 0), (2, 1), (2, 2), (3, 0), (3, 1), (3, 2), (3, 3))
VMEM = pl.BlockSpec(memory_space=pltpu.VMEM)
SMEM = pl.BlockSpec(memory_space=pltpu.SMEM)
PARAMS = pltpu.CompilerParams(vmem_limit_bytes=32 * 1024 * 1024)
WIDE = pltpu.CompilerParams(vmem_limit_bytes=60 * 1024 * 1024)


def split2(x):
    hi = x.astype(jnp.bfloat16)
    return hi, (x - hi.astype(jnp.float32)).astype(jnp.bfloat16)


def left(x):
    hi, lo = split2(x)
    return jnp.concatenate([hi, hi, lo], axis=1)


def right(x):
    hi, lo = split2(x)
    return jnp.concatenate([hi, lo, hi], axis=1)


def dot_t(a, b):
    return lax.dot_general(a, b, (((1,), (1,)), ((), ())), preferred_element_type=jnp.float32)


def factor_block(rows, c_ref, u_ref, w_ref):
    lane = lax.broadcasted_iota(jnp.int32, (8, BLOCK), 1)
    sub = lax.broadcasted_iota(jnp.int32, (8, BLOCK), 0)
    rows = list(rows)
    groups = len(rows)
    full = (8, BLOCK)
    for k in range(groups):
        base = k * 8
        own = (lane >= base) & (lane < base + 8)
        panel = rows[k]
        for j in range(8):
            c_ref[k % 2, j] = jnp.broadcast_to(panel[:, base + j : base + j + 1], full)
        c_ref[k % 2, 8] = panel
        spread = lambda j, i: jnp.broadcast_to(c_ref[k % 2, j, i : i + 1, :], full)
        piv = {(i, j): spread(j, i) for i in range(8) for j in range(i + 1)}
        root, inv, low, ratio = {}, {}, {}, {}
        for j in range(0, 8, 2):
            x, y, z = piv[j, j], piv[j + 1, j], piv[j + 1, j + 1]
            det = x * z - y * y
            rd = 1.0 / det
            for i in range(j + 2, 8):
                p, q = piv[i, j], piv[i, j + 1]
                f, g = p * z - q * y, q * x - p * y
                low[i, j], low[i, j + 1] = f * rd, g * rd
                for m in range(j + 2, i + 1):
                    if i < j + 4:
                        piv[i, m] = piv[i, m] - (f * piv[m, j] + g * piv[m, j + 1]) * rd
                    else:
                        piv[i, m] = piv[i, m] - low[i, j] * piv[m, j] - low[i, j + 1] * piv[m, j + 1]
            inv[j] = (z * rd, y * rd, x * rd)
            root[j] = lax.rsqrt(x)
            root[j + 1] = lax.rsqrt(det) * (x * root[j])
            ratio[j] = y * (root[j] * root[j])
        fwd, fwd_u = [], []
        for i in range(8):
            u = spread(8, i)
            w = jnp.where(own, jnp.where(lane == base + i, 1.0, 0.0), u)
            for j in range(i - i % 2):
                w = w - low[i, j] * fwd[j]
                u = u - low[i, j] * fwd_u[j]
            fwd.append(w)
            fwd_u.append(u)
        back = [None] * 8
        for i in reversed(range(0, 8, 2)):
            f, g = fwd[i], fwd[i + 1]
            x, y, z = inv[i]
            v, w = f * x - g * y, g * z - f * y
            for j in range(i + 2, 8):
                v = v - low[j, i] * back[j]
                w = w - low[j, i + 1] * back[j]
            back[i], back[i + 1] = v, w
        if k + 1 < groups:
            part, near = jnp.where(own, 0.0, rows[k + 1]), []
            for i in range(8):
                u = jnp.broadcast_to(rows[k + 1][:, base + i : base + i + 1], full)
                for j in range(i - i % 2):
                    u = u - low[i, j] * near[j]
                near.append(u)
            for i in range(0, 8, 2):
                x, y, z = inv[i]
                v, w = fwd[i] * x - fwd[i + 1] * y, fwd[i + 1] * z - fwd[i] * y
                part = part - (near[i] * v + near[i + 1] * w)
            rows[k + 1] = part
        for r in range(k + 2, groups):
            terms = [jnp.broadcast_to(rows[r][:, base + j : base + j + 1], full) * back[j] for j in range(8)]
            while len(terms) > 1:
                terms = [x + y for x, y in zip(terms[::2], terms[1::2])]
            rows[r] = jnp.where(own, 0.0, rows[r]) - terms[0]
        for g in range(8):
            h = g - g % 2
            w = fwd[g] if g == h else fwd[g] - ratio[h] * fwd[h]
            u = fwd_u[g] if g == h else fwd_u[g] - ratio[h] * fwd_u[h]
            u_ref[base + g : base + g + 1, :] = jnp.where(lane >= base + g, u * root[g], 0.0)[:1, :]
            w_ref[base + g : base + g + 1, :] = jnp.where(lane <= base + g, w * root[g], 0.0)[:1, :]


def chol_kernel(core_ref, own_ref, other_ref, x_ref, l_out, o_out, a_ref, l_ref, o_ref, c_ref, u_ref, w_ref, sems):
    n = x_ref.shape[1]
    nb = n // BLOCK
    at = [slice(k * BLOCK, (k + 1) * BLOCK) for k in range(nb)]
    r = lax.broadcasted_iota(jnp.int32, (BLOCK, BLOCK), 0)
    c = lax.broadcasted_iota(jnp.int32, (BLOCK, BLOCK), 1)
    row_scale, col_scale, row_root = [], [], []
    copies = []
    gram = lambda i, j: lower_block(core_ref[0], own_ref, other_ref, i, j)
    for k in range(nb):
        diag = jnp.where(r == c, gram(k, k), 0.0)
        by_row = jnp.broadcast_to(jnp.sum(diag, axis=1, keepdims=True), (BLOCK, BLOCK))
        s = lax.rsqrt(by_row)
        row_scale.append(s)
        row_root.append(by_row * s)
        col_scale.append(lax.rsqrt(jnp.sum(diag, axis=0, keepdims=True)))
    for k in range(nb):
        for i in range(k, nb):
            a_ref[at[i], at[k]] = gram(i, k) * row_scale[i] * col_scale[k]
    for k in range(nb):
        panels = [a_ref[k * BLOCK + p * 8 : k * BLOCK + (p + 1) * 8, at[k]] for p in range(BLOCK // 8)]
        factor_block(panels, c_ref, u_ref.at[k % 2], w_ref.at[k % 2])
        ws = right(w_ref[k % 2])
        below = {}
        for i in range(k + 1, nb):
            below[i] = dot_t(left(a_ref[at[i], at[k]]), ws)
            for j in range(k + 1, i + 1):
                a_ref[at[i], at[j]] = a_ref[at[i], at[j]] - dot_t(left(below[i]), right(below[j]))
        before = x_ref[:, at[k]] * col_scale[k]
        if k:
            before = before - o_ref[:, at[k]]
        solved = dot_t(left(before), ws)
        o_ref[:, at[k]] = solved
        for i in range(k + 1, nb):
            add = dot_t(left(solved), right(below[i]))
            o_ref[:, at[i]] = o_ref[:, at[i]] + add if k else add
        for i in range(k):
            l_ref[at[i], at[k]] = jnp.zeros((BLOCK, BLOCK), jnp.float32)
        l_ref[at[k], at[k]] = u_ref[k % 2].T * row_root[k]
        for i in range(k + 1, nb):
            l_ref[at[i], at[k]] = below[i] * row_root[i]
        copies.append(pltpu.make_async_copy(o_ref.at[:, at[k]], o_out.at[:, at[k]], sems.at[2 * k]))
        copies.append(pltpu.make_async_copy(l_ref.at[:, at[k]], l_out.at[:, at[k]], sems.at[2 * k + 1]))
        copies[-2].start()
        copies[-1].start()
    for copy in copies:
        copy.wait()


def lower_block(core, own_ref, other_ref, i, j):
    half, slot = divmod(LOWER.index((i, j)), len(LOWER) // 2)
    mine = jnp.broadcast_to(core, (8, BLOCK)) == half
    at = slice(slot * 8, slot * 8 + 8)
    parts = [jnp.where(mine, own_ref[chip, at, :], other_ref[chip, at, :]) for chip in range(BLOCK // 8)]
    return jnp.concatenate(parts, axis=0)


def chol_solve(core, own, other, x):
    rows, n = x.shape
    return pl.pallas_call(
        chol_kernel,
        out_shape=(jax.ShapeDtypeStruct((n, n), jnp.float32), jax.ShapeDtypeStruct(x.shape, jnp.float32)),
        in_specs=[SMEM, VMEM, VMEM, VMEM],
        out_specs=[pl.BlockSpec(memory_space=pl.ANY)] * 2,
        scratch_shapes=[
            pltpu.VMEM((n, n), jnp.float32),
            pltpu.VMEM((n, n), jnp.float32),
            pltpu.VMEM((rows, n), jnp.float32),
            pltpu.VMEM((2, 9, 8, BLOCK), jnp.float32),
            pltpu.VMEM((2, BLOCK, BLOCK), jnp.float32),
            pltpu.VMEM((2, BLOCK, BLOCK), jnp.float32),
            pltpu.SemaphoreType.DMA((2 * (n // BLOCK),)),
        ],
        compiler_params=PARAMS,
    )(core.reshape(1), own, other, x)


def gram_kernel(chip_ref, p_ref, o_ref):
    blocks = p_ref.shape[0] // BLOCK
    first = chip_ref[0] * 8
    rows = [p_ref[pl.ds(pl.multiple_of(i * BLOCK + first, 8), 8), :] for i in range(blocks)]
    product = dot_t(left(jnp.concatenate(rows, axis=0)), right(p_ref[...]))
    for t, (i, j) in enumerate(LOWER):
        o_ref[t * 8 : t * 8 + 8, :] = product[i * 8 : i * 8 + 8, j * BLOCK : (j + 1) * BLOCK]


def gram_part(columns, chip):
    return pl.pallas_call(
        gram_kernel,
        out_shape=jax.ShapeDtypeStruct((8 * len(LOWER), BLOCK), jnp.float32),
        in_specs=[SMEM, VMEM],
        out_specs=VMEM,
        compiler_params=PARAMS,
    )(chip.reshape(1), columns)


def flip_kernel(x_ref, signs_ref, o_ref, buf_ref, row_ref, sems):
    rows, n = buf_ref.shape
    parts = rows // BLOCK
    sign_copy = pltpu.make_async_copy(signs_ref, row_ref, sems.at[parts])
    copies = []
    for k in range(parts):
        at = pl.ds(k * BLOCK, BLOCK)
        copies.append(pltpu.make_async_copy(x_ref.at[at, :], buf_ref.at[at, :], sems.at[k]))
    copies[0].start()
    sign_copy.start()
    for copy in copies[1:]:
        copy.start()
    sign_copy.wait()
    for k in range(parts):
        copies[k].wait()
        at = slice(k * BLOCK, (k + 1) * BLOCK)
        sign = row_ref[:, at].astype(jnp.float32)
        for c in range(n // BLOCK):
            cols = slice(c * BLOCK, (c + 1) * BLOCK)
            o_ref[cols, at] = buf_ref[at, cols].T * sign


def signed_columns(matrix, signs):
    rows, n = matrix.shape
    hbm = pl.BlockSpec(memory_space=pl.ANY)
    return pl.pallas_call(
        flip_kernel,
        out_shape=jax.ShapeDtypeStruct((n, rows), jnp.float32),
        in_specs=[hbm, hbm],
        out_specs=VMEM,
        scratch_shapes=[
            pltpu.VMEM((rows, n), jnp.float32),
            pltpu.VMEM((1, rows), jnp.int32),
            pltpu.SemaphoreType.DMA((rows // BLOCK + 1,)),
        ],
        compiler_params=WIDE,
    )(matrix, signs.reshape(1, -1))


def signs_of(value, count):
    v = lax.broadcasted_iota(jnp.int32, (count, value.shape[1]), 0) & value
    for shift in (4, 2, 1):
        v = v ^ (v >> shift)
    return (1 - 2 * (v & 1)).astype(jnp.float32)


def mix_kernel(pos_ref, x_ref, samples_ref, o_ref, h_ref):
    width = x_ref.shape[0]
    depth = x_ref.shape[1]
    sources = 32
    cols = width // sources
    hi, lo = split2(x_ref[...])
    z_bits = pos_ref[0]
    scale = 1.0 / 512.0
    for c in range(samples_ref.shape[1] // CHUNK):
        s = samples_ref[:, c * CHUNK : (c + 1) * CHUNK]
        within = s & (depth - 1)
        device = s // depth
        low = signs_of(within & 15, 16)
        high = signs_of(within // 16, depth // 16)
        for r in range(depth // 16):
            h_ref[r * 16 : (r + 1) * 16, :] = (low * high[r : r + 1, :]).astype(jnp.bfloat16)
        plane_sign = signs_of((device & 15) | ((device // 256) * 16), sources)
        zv = (device // 16) & z_bits
        zv = zv ^ (zv >> 2)
        zv = zv ^ (zv >> 1)
        z_sign = (1 - 2 * (zv & 1)).astype(jnp.float32) * scale
        h = h_ref[...]
        t = jnp.dot(hi, h, preferred_element_type=jnp.float32)
        t = t + jnp.dot(lo, h, preferred_element_type=jnp.float32)
        acc = t[:cols, :]
        for p in range(1, sources):
            acc = acc + t[p * cols : (p + 1) * cols, :] * plane_sign[p : p + 1, :]
        acc = acc * z_sign
        for b in range(CHUNK // SHARE):
            o_ref[c * (CHUNK // SHARE) + b] = acc[:, b * SHARE : (b + 1) * SHARE]


def sample_columns(columns, samples, z_index):
    width = columns.shape[0]
    count = samples.shape[0]
    return pl.pallas_call(
        mix_kernel,
        out_shape=jax.ShapeDtypeStruct((count // SHARE, width // 32, SHARE), jnp.float32),
        in_specs=[SMEM, VMEM, VMEM],
        out_specs=VMEM,
        scratch_shapes=[pltpu.VMEM((columns.shape[1], CHUNK), jnp.bfloat16)],
        compiler_params=PARAMS,
    )(z_index.reshape(1), columns, samples.reshape(1, count))


def fan_kernel(x_ref, o_ref):
    total = jnp.sum(x_ref[...], axis=0)
    for i in range(o_ref.shape[0]):
        o_ref[i] = total


def fan_out(blocks, count):
    return pl.pallas_call(
        fan_kernel,
        out_shape=jax.ShapeDtypeStruct((count,) + blocks.shape[1:], jnp.float32),
        in_specs=[VMEM],
        out_specs=VMEM,
        compiler_params=PARAMS,
    )(blocks)


def exchange(block, axes):
    return lax.all_to_all(block, axes, 0, 0, tiled=True)


def gather(block, axes):
    count = lax.axis_size(axes)
    return exchange(jnp.broadcast_to(block[None], (count,) + block.shape), axes)


def body(matrix, signs, samples):
    rows, n = matrix.shape
    plane = lax.axis_size(PLANE)
    core = lax.axis_index("core")
    columns = exchange(signed_columns(matrix, signs).reshape(plane, n // plane, rows), PLANE)
    partial = sample_columns(columns.reshape(n, rows), samples, lax.axis_index(("z_hi", "z_lo")))
    mine = exchange(partial, NEAR).reshape(lax.axis_size("z_lo"), 2 * (n // plane), -1)
    mine = fan_out(gather(jnp.sum(mine, axis=0), "z_hi"), lax.axis_size(CHIPS))
    every = exchange(mine, CHIPS).reshape(n, -1)
    part = gram_part(every, lax.axis_index(CHIPS)).reshape(1, 2, 4 * len(LOWER), BLOCK)
    part = jnp.broadcast_to(part, (lax.axis_size("z_lo"),) + part.shape[1:])
    part = jnp.sum(exchange(part.reshape((-1,) + part.shape[2:]), NEAR), axis=0) / jnp.float32(samples.shape[0])
    own = gather(part, CHIPS)
    other = lax.ppermute(own, "core", [(0, 1), (1, 0)])
    return chol_solve(core, own, other, matrix)


def solution(mesh):
    fine = Mesh(mesh.devices.reshape(2, 4, 4, 2, 4, 2), ROW_AXES)
    in_specs = (P(ROW_AXES, None), P(ROW_AXES), P())
    out_specs = (P(), P(ROW_AXES, None))
    return jax.shard_map(body, mesh=fine, in_specs=in_specs, out_specs=out_specs, check_vma=False)
```

```python
import jax
import jax.numpy as jnp
from jax import lax
from jax.experimental import pallas as pl
from jax.experimental.pallas import tpu as pltpu
from jax.sharding import Mesh
from jax.sharding import PartitionSpec as P

BLOCK = 128
CHUNK = 512
SHARE = 256
ROW_AXES = ("x_hi", "z_hi", "z_lo", "x_lo", "y", "core")
PLANE = ("x_hi", "x_lo", "y", "core")
CHIPS = ("x_hi", "x_lo", "y")
NEAR = ("z_lo", "core")
LOWER = ((0, 0), (1, 0), (1, 1), (2, 0), (2, 1), (2, 2), (3, 0), (3, 1), (3, 2), (3, 3))
VMEM = pl.BlockSpec(memory_space=pltpu.VMEM)
SMEM = pl.BlockSpec(memory_space=pltpu.SMEM)
PARAMS = pltpu.CompilerParams(vmem_limit_bytes=32 * 1024 * 1024)
WIDE = pltpu.CompilerParams(vmem_limit_bytes=60 * 1024 * 1024)


def split2(x):
    hi = x.astype(jnp.bfloat16)
    return hi, (x - hi.astype(jnp.float32)).astype(jnp.bfloat16)


def left(x):
    hi, lo = split2(x)
    return jnp.concatenate([hi, hi, lo], axis=1)


def right(x):
    hi, lo = split2(x)
    return jnp.concatenate([hi, lo, hi], axis=1)


def dot_t(a, b):
    return lax.dot_general(a, b, (((1,), (1,)), ((), ())), preferred_element_type=jnp.float32)


def factor_block(rows, c_ref, u_ref, w_ref):
    lane = lax.broadcasted_iota(jnp.int32, (8, BLOCK), 1)
    sub = lax.broadcasted_iota(jnp.int32, (8, BLOCK), 0)
    rows = list(rows)
    groups = len(rows)
    full = (8, BLOCK)
    for k in range(groups):
        base = k * 8
        own = (lane >= base) & (lane < base + 8)
        for j in range(8):
            c_ref[k % 2, j] = jnp.broadcast_to(rows[0][:, j : j + 1], full) if k == 0 else ahead[j]
        c_ref[k % 2, 8] = rows[k]
        spread = lambda j, i: jnp.broadcast_to(c_ref[k % 2, j, i : i + 1, :], full)
        piv = {(i, j): spread(j, i) for i in range(8) for j in range(i + 1)}
        root, inv, low, ratio = {}, {}, {}, {}
        for j in range(0, 8, 2):
            x, y, z = piv[j, j], piv[j + 1, j], piv[j + 1, j + 1]
            det = x * z - y * y
            rd = 1.0 / det
            for i in range(j + 2, 8):
                p, q = piv[i, j], piv[i, j + 1]
                f, g = p * z - q * y, q * x - p * y
                low[i, j], low[i, j + 1] = f * rd, g * rd
                for m in range(j + 2, i + 1):
                    if i < j + 4:
                        piv[i, m] = piv[i, m] - (f * piv[m, j] + g * piv[m, j + 1]) * rd
                    else:
                        piv[i, m] = piv[i, m] - low[i, j] * piv[m, j] - low[i, j + 1] * piv[m, j + 1]
            inv[j] = (z * rd, y * rd, x * rd)
            root[j] = lax.rsqrt(x)
            root[j + 1] = lax.rsqrt(det) * (x * root[j])
            ratio[j] = y * (root[j] * root[j])
        fwd, fwd_u = [], []
        for i in range(8):
            u = spread(8, i)
            w = jnp.where(own, jnp.where(lane == base + i, 1.0, 0.0), u)
            for j in range(i - i % 2):
                w = w - low[i, j] * fwd[j]
                u = u - low[i, j] * fwd_u[j]
            fwd.append(w)
            fwd_u.append(u)
        back = [None] * 8
        for i in reversed(range(0, 8, 2)):
            f, g = fwd[i], fwd[i + 1]
            x, y, z = inv[i]
            v, w = f * x - g * y, g * z - f * y
            for j in range(i + 2, 8):
                v = v - low[j, i] * back[j]
                w = w - low[j, i + 1] * back[j]
            back[i], back[i + 1] = v, w
        if k + 1 < groups:
            part, near = jnp.where(own, 0.0, rows[k + 1]), []
            ahead = [jnp.broadcast_to(rows[k + 1][:, base + 8 + j : base + 9 + j], full) for j in range(8)]
            for i in range(8):
                u = jnp.broadcast_to(rows[k + 1][:, base + i : base + i + 1], full)
                for j in range(i - i % 2):
                    u = u - low[i, j] * near[j]
                near.append(u)
            for i in range(0, 8, 2):
                x, y, z = inv[i]
                v, w = fwd[i] * x - fwd[i + 1] * y, fwd[i + 1] * z - fwd[i] * y
                part = part - (near[i] * v + near[i + 1] * w)
                c_ref[k % 2, 9 + i] = near[i] * x - near[i + 1] * y
                c_ref[k % 2, 10 + i] = near[i + 1] * z - near[i] * y
                for j in range(8):
                    ahead[j] = ahead[j] - (near[i] * spread(9 + i, j) + near[i + 1] * spread(10 + i, j))
            rows[k + 1] = part
        for r in range(k + 2, groups):
            terms = [jnp.broadcast_to(rows[r][:, base + j : base + j + 1], full) * back[j] for j in range(8)]
            while len(terms) > 1:
                terms = [x + y for x, y in zip(terms[::2], terms[1::2])]
            rows[r] = jnp.where(own, 0.0, rows[r]) - terms[0]
        for g in range(8):
            h = g - g % 2
            w = fwd[g] if g == h else fwd[g] - ratio[h] * fwd[h]
            u = fwd_u[g] if g == h else fwd_u[g] - ratio[h] * fwd_u[h]
            u_ref[base + g : base + g + 1, :] = jnp.where(lane >= base + g, u * root[g], 0.0)[:1, :]
            w_ref[base + g : base + g + 1, :] = jnp.where(lane <= base + g, w * root[g], 0.0)[:1, :]


def chol_kernel(core_ref, own_ref, other_ref, x_ref, l_out, o_out, a_ref, l_ref, o_ref, c_ref, u_ref, w_ref, sems):
    n = x_ref.shape[1]
    nb = n // BLOCK
    at = [slice(k * BLOCK, (k + 1) * BLOCK) for k in range(nb)]
    r = lax.broadcasted_iota(jnp.int32, (BLOCK, BLOCK), 0)
    c = lax.broadcasted_iota(jnp.int32, (BLOCK, BLOCK), 1)
    row_scale, col_scale, row_root = [], [], []
    copies = []
    gram = lambda i, j: lower_block(core_ref[0], own_ref, other_ref, i, j)
    for k in range(nb):
        diag = jnp.where(r == c, gram(k, k), 0.0)
        by_row = jnp.broadcast_to(jnp.sum(diag, axis=1, keepdims=True), (BLOCK, BLOCK))
        s = lax.rsqrt(by_row)
        row_scale.append(s)
        row_root.append(by_row * s)
        col_scale.append(lax.rsqrt(jnp.sum(diag, axis=0, keepdims=True)))
    for k in range(nb):
        for i in range(k, nb):
            a_ref[at[i], at[k]] = gram(i, k) * row_scale[i] * col_scale[k]
    for k in range(nb):
        panels = [a_ref[k * BLOCK + p * 8 : k * BLOCK + (p + 1) * 8, at[k]] for p in range(BLOCK // 8)]
        factor_block(panels, c_ref, u_ref.at[k % 2], w_ref.at[k % 2])
        ws = right(w_ref[k % 2])
        below = {}
        for i in range(k + 1, nb):
            below[i] = dot_t(left(a_ref[at[i], at[k]]), ws)
            for j in range(k + 1, i + 1):
                a_ref[at[i], at[j]] = a_ref[at[i], at[j]] - dot_t(left(below[i]), right(below[j]))
        before = x_ref[:, at[k]] * col_scale[k]
        if k:
            before = before - o_ref[:, at[k]]
        solved = dot_t(left(before), ws)
        o_ref[:, at[k]] = solved
        for i in range(k + 1, nb):
            add = dot_t(left(solved), right(below[i]))
            o_ref[:, at[i]] = o_ref[:, at[i]] + add if k else add
        for i in range(k):
            l_ref[at[i], at[k]] = jnp.zeros((BLOCK, BLOCK), jnp.float32)
        l_ref[at[k], at[k]] = u_ref[k % 2].T * row_root[k]
        for i in range(k + 1, nb):
            l_ref[at[i], at[k]] = below[i] * row_root[i]
        copies.append(pltpu.make_async_copy(o_ref.at[:, at[k]], o_out.at[:, at[k]], sems.at[2 * k]))
        copies.append(pltpu.make_async_copy(l_ref.at[:, at[k]], l_out.at[:, at[k]], sems.at[2 * k + 1]))
        copies[-2].start()
        copies[-1].start()
    for copy in copies:
        copy.wait()


def lower_block(core, own_ref, other_ref, i, j):
    half, slot = divmod(LOWER.index((i, j)), len(LOWER) // 2)
    mine = jnp.broadcast_to(core, (8, BLOCK)) == half
    at = slice(slot * 8, slot * 8 + 8)
    parts = [jnp.where(mine, own_ref[chip, at, :], other_ref[chip, at, :]) for chip in range(BLOCK // 8)]
    return jnp.concatenate(parts, axis=0)


def chol_solve(core, own, other, x):
    rows, n = x.shape
    return pl.pallas_call(
        chol_kernel,
        out_shape=(jax.ShapeDtypeStruct((n, n), jnp.float32), jax.ShapeDtypeStruct(x.shape, jnp.float32)),
        in_specs=[SMEM, VMEM, VMEM, VMEM],
        out_specs=[pl.BlockSpec(memory_space=pl.ANY)] * 2,
        scratch_shapes=[
            pltpu.VMEM((n, n), jnp.float32),
            pltpu.VMEM((n, n), jnp.float32),
            pltpu.VMEM((rows, n), jnp.float32),
            pltpu.VMEM((2, 17, 8, BLOCK), jnp.float32),
            pltpu.VMEM((2, BLOCK, BLOCK), jnp.float32),
            pltpu.VMEM((2, BLOCK, BLOCK), jnp.float32),
            pltpu.SemaphoreType.DMA((2 * (n // BLOCK),)),
        ],
        compiler_params=PARAMS,
    )(core.reshape(1), own, other, x)


def gram_kernel(chip_ref, p_ref, o_ref, all_ref):
    blocks = all_ref.shape[0] // BLOCK
    half = p_ref.shape[2] // 2
    for chip in range(p_ref.shape[0]):
        for core in range(2):
            all_ref[chip * 32 + core * 16 : chip * 32 + core * 16 + 16, :] = p_ref[chip, :, core * half : (core + 1) * half]
    first = chip_ref[0] * 8
    rows = [all_ref[pl.ds(pl.multiple_of(i * BLOCK + first, 8), 8), :] for i in range(blocks)]
    product = dot_t(left(jnp.concatenate(rows, axis=0)), right(all_ref[...]))
    for t, (i, j) in enumerate(LOWER):
        o_ref[t * 8 : t * 8 + 8, :] = product[i * 8 : i * 8 + 8, j * BLOCK : (j + 1) * BLOCK]


def gram_part(columns, chip):
    chips, group, depth = columns.shape
    return pl.pallas_call(
        gram_kernel,
        out_shape=jax.ShapeDtypeStruct((8 * len(LOWER), BLOCK), jnp.float32),
        in_specs=[SMEM, VMEM],
        out_specs=VMEM,
        scratch_shapes=[pltpu.VMEM((2 * chips * group, depth // 2), jnp.float32)],
        compiler_params=PARAMS,
    )(chip.reshape(1), columns)


def flip_kernel(x_ref, signs_ref, o_ref, buf_ref, row_ref, t_ref, sems):
    rows, n = buf_ref.shape
    parts = rows // BLOCK
    sign_copy = pltpu.make_async_copy(signs_ref, row_ref, sems.at[2 * parts])
    loads, stores = [], []
    for k in range(parts):
        at = pl.ds(k * BLOCK, BLOCK)
        loads.append(pltpu.make_async_copy(x_ref.at[at, :], buf_ref.at[at, :], sems.at[k]))
        stores.append(pltpu.make_async_copy(t_ref.at[:, at], o_ref.at[:, at], sems.at[parts + k]))
    loads[0].start()
    sign_copy.start()
    for load in loads[1:]:
        load.start()
    sign_copy.wait()
    for k in range(parts):
        loads[k].wait()
        at = slice(k * BLOCK, (k + 1) * BLOCK)
        sign = row_ref[:, at].astype(jnp.float32)
        for c in range(n // BLOCK):
            cols = slice(c * BLOCK, (c + 1) * BLOCK)
            t_ref[cols, at] = buf_ref[at, cols].T * sign
        stores[k].start()
    for store in stores:
        store.wait()


def signed_columns(matrix, signs):
    rows, n = matrix.shape
    hbm = pl.BlockSpec(memory_space=pl.ANY)
    return pl.pallas_call(
        flip_kernel,
        out_shape=jax.ShapeDtypeStruct((n, rows), jnp.float32),
        in_specs=[hbm, hbm],
        out_specs=hbm,
        scratch_shapes=[
            pltpu.VMEM((rows, n), jnp.float32),
            pltpu.VMEM((1, rows), jnp.int32),
            pltpu.VMEM((n, rows), jnp.float32),
            pltpu.SemaphoreType.DMA((2 * (rows // BLOCK) + 1,)),
        ],
        compiler_params=WIDE,
    )(matrix, signs.reshape(1, -1))


def signs_of(value, count):
    v = lax.broadcasted_iota(jnp.int32, (count, value.shape[1]), 0) & value
    for shift in (4, 2, 1):
        v = v ^ (v >> shift)
    return (1 - 2 * (v & 1)).astype(jnp.float32)


def mix_kernel(pos_ref, x_ref, samples_ref, o_ref, h_ref):
    width = x_ref.shape[0]
    depth = x_ref.shape[1]
    sources = 32
    cols = width // sources
    hi, lo = split2(x_ref[...])
    z_bits = pos_ref[0]
    scale = 1.0 / 512.0
    for c in range(samples_ref.shape[1] // CHUNK):
        s = samples_ref[:, c * CHUNK : (c + 1) * CHUNK]
        within = s & (depth - 1)
        device = s // depth
        low = signs_of(within & 15, 16)
        high = signs_of(within // 16, depth // 16)
        for r in range(depth // 16):
            h_ref[r * 16 : (r + 1) * 16, :] = (low * high[r : r + 1, :]).astype(jnp.bfloat16)
        plane_sign = signs_of((device & 15) | ((device // 256) * 16), sources)
        zv = (device // 16) & z_bits
        zv = zv ^ (zv >> 2)
        zv = zv ^ (zv >> 1)
        z_sign = (1 - 2 * (zv & 1)).astype(jnp.float32) * scale
        h = h_ref[...]
        t = jnp.dot(hi, h, preferred_element_type=jnp.float32)
        t = t + jnp.dot(lo, h, preferred_element_type=jnp.float32)
        acc = t[:cols, :]
        for p in range(1, sources):
            acc = acc + t[p * cols : (p + 1) * cols, :] * plane_sign[p : p + 1, :]
        acc = acc * z_sign
        for b in range(CHUNK // SHARE):
            o_ref[c * (CHUNK // SHARE) + b] = acc[:, b * SHARE : (b + 1) * SHARE]


def sample_columns(columns, samples, z_index):
    width = columns.shape[0]
    count = samples.shape[0]
    return pl.pallas_call(
        mix_kernel,
        out_shape=jax.ShapeDtypeStruct((count // SHARE, width // 32, SHARE), jnp.float32),
        in_specs=[SMEM, VMEM, VMEM],
        out_specs=VMEM,
        scratch_shapes=[pltpu.VMEM((columns.shape[1], CHUNK), jnp.bfloat16)],
        compiler_params=PARAMS,
    )(z_index.reshape(1), columns, samples.reshape(1, count))


def near_kernel(x_ref, o_ref):
    half = x_ref.shape[2]
    for core in range(2):
        total = x_ref[core]
        for z in range(1, x_ref.shape[0] // 2):
            total = total + x_ref[2 * z + core]
        o_ref[:, core * half : (core + 1) * half] = total


def near_sum(blocks):
    return pl.pallas_call(
        near_kernel,
        out_shape=jax.ShapeDtypeStruct((blocks.shape[1], 2 * blocks.shape[2]), jnp.float32),
        in_specs=[VMEM],
        out_specs=VMEM,
        compiler_params=PARAMS,
    )(blocks)


def exchange(block, axes):
    return lax.all_to_all(block, axes, 0, 0, tiled=True)


def gather(block, axes):
    count = lax.axis_size(axes)
    return exchange(jnp.broadcast_to(block[None], (count,) + block.shape), axes)


def body(matrix, signs, samples):
    rows, n = matrix.shape
    plane = lax.axis_size(PLANE)
    core = lax.axis_index("core")
    columns = exchange(signed_columns(matrix, signs).reshape(plane, n // plane, rows), PLANE)
    partial = sample_columns(columns.reshape(n, rows), samples, lax.axis_index(("z_hi", "z_lo")))
    mine = near_sum(exchange(partial, NEAR))
    mine = jnp.sum(gather(mine, "z_hi"), axis=0)
    every = gather(mine, CHIPS)
    part = gram_part(every, lax.axis_index(CHIPS)).reshape(1, 2, 4 * len(LOWER), BLOCK)
    part = jnp.broadcast_to(part, (lax.axis_size("z_lo"),) + part.shape[1:])
    part = jnp.sum(exchange(part.reshape((-1,) + part.shape[2:]), NEAR), axis=0) / jnp.float32(samples.shape[0])
    own = gather(part, CHIPS)
    other = lax.ppermute(own, "core", [(0, 1), (1, 0)])
    return chol_solve(core, own, other, matrix)


def solution(mesh):
    fine = Mesh(mesh.devices.reshape(2, 4, 4, 2, 4, 2), ROW_AXES)
    in_specs = (P(ROW_AXES, None), P(ROW_AXES), P())
    out_specs = (P(), P(ROW_AXES, None))
    return jax.shard_map(body, mesh=fine, in_specs=in_specs, out_specs=out_specs, check_vma=False)
```

```python
import jax
import jax.numpy as jnp
from jax import lax
from jax.experimental import pallas as pl
from jax.experimental.pallas import tpu as pltpu
from jax.sharding import Mesh
from jax.sharding import PartitionSpec as P

BLOCK = 128
CHUNK = 512
SHARE = 256
ROW_AXES = ("x_hi", "z_hi", "z_lo", "x_lo", "y", "core")
PLANE = ("x_hi", "x_lo", "y", "core")
CHIPS = ("x_hi", "x_lo", "y")
NEAR = ("z_lo", "core")
LOWER = ((0, 0), (1, 0), (1, 1), (2, 0), (2, 1), (2, 2), (3, 0), (3, 1), (3, 2), (3, 3))
VMEM = pl.BlockSpec(memory_space=pltpu.VMEM)
SMEM = pl.BlockSpec(memory_space=pltpu.SMEM)
PARAMS = pltpu.CompilerParams(vmem_limit_bytes=32 * 1024 * 1024)
WIDE = pltpu.CompilerParams(vmem_limit_bytes=60 * 1024 * 1024)


def split2(x):
    hi = x.astype(jnp.bfloat16)
    return hi, (x - hi.astype(jnp.float32)).astype(jnp.bfloat16)


def left(x):
    hi, lo = split2(x)
    return jnp.concatenate([hi, hi, lo], axis=1)


def right(x):
    hi, lo = split2(x)
    return jnp.concatenate([hi, lo, hi], axis=1)


def dot_t(a, b):
    return lax.dot_general(a, b, (((1,), (1,)), ((), ())), preferred_element_type=jnp.float32)


def factor_block(rows, c_ref, u_ref, w_ref):
    lane = lax.broadcasted_iota(jnp.int32, (8, BLOCK), 1)
    sub = lax.broadcasted_iota(jnp.int32, (8, BLOCK), 0)
    rows = list(rows)
    groups = len(rows)
    full = (8, BLOCK)
    for k in range(groups):
        base = k * 8
        own = (lane >= base) & (lane < base + 8)
        for j in range(8):
            c_ref[k % 2, j] = jnp.broadcast_to(rows[0][:, j : j + 1], full) if k == 0 else ahead[j]
        c_ref[k % 2, 8] = rows[k]
        spread = lambda j, i: jnp.broadcast_to(c_ref[k % 2, j, i : i + 1, :], full)
        piv = {(i, j): spread(j, i) for i in range(8) for j in range(i + 1)}
        root, inv, low, ratio = {}, {}, {}, {}
        for j in range(0, 8, 2):
            x, y, z = piv[j, j], piv[j + 1, j], piv[j + 1, j + 1]
            det = x * z - y * y
            rd = 1.0 / det
            for i in range(j + 2, 8):
                p, q = piv[i, j], piv[i, j + 1]
                f, g = p * z - q * y, q * x - p * y
                low[i, j], low[i, j + 1] = f * rd, g * rd
                for m in range(j + 2, i + 1):
                    if i < j + 4:
                        piv[i, m] = piv[i, m] - (f * piv[m, j] + g * piv[m, j + 1]) * rd
                    else:
                        piv[i, m] = piv[i, m] - low[i, j] * piv[m, j] - low[i, j + 1] * piv[m, j + 1]
            inv[j] = (z * rd, y * rd, x * rd)
            root[j] = lax.rsqrt(x)
            root[j + 1] = lax.rsqrt(det) * (x * root[j])
            ratio[j] = y * (root[j] * root[j])
        fwd, fwd_u = [], []
        for i in range(8):
            u = spread(8, i)
            w = jnp.where(own, jnp.where(lane == base + i, 1.0, 0.0), u)
            for j in range(i - i % 2):
                w = w - low[i, j] * fwd[j]
                u = u - low[i, j] * fwd_u[j]
            fwd.append(w)
            fwd_u.append(u)
        back = [None] * 8
        for i in reversed(range(0, 8, 2)):
            f, g = fwd[i], fwd[i + 1]
            x, y, z = inv[i]
            v, w = f * x - g * y, g * z - f * y
            for j in range(i + 2, 8):
                v = v - low[j, i] * back[j]
                w = w - low[j, i + 1] * back[j]
            back[i], back[i + 1] = v, w
        if k + 1 < groups:
            part, near = jnp.where(own, 0.0, rows[k + 1]), []
            ahead = [jnp.broadcast_to(rows[k + 1][:, base + 8 + j : base + 9 + j], full) for j in range(8)]
            for i in range(8):
                u = jnp.broadcast_to(rows[k + 1][:, base + i : base + i + 1], full)
                for j in range(i - i % 2):
                    u = u - low[i, j] * near[j]
                near.append(u)
            for i in range(0, 8, 2):
                x, y, z = inv[i]
                v, w = fwd[i] * x - fwd[i + 1] * y, fwd[i + 1] * z - fwd[i] * y
                part = part - (near[i] * v + near[i + 1] * w)
                c_ref[k % 2, 9 + i] = near[i] * x - near[i + 1] * y
                c_ref[k % 2, 10 + i] = near[i + 1] * z - near[i] * y
                for j in range(8):
                    ahead[j] = ahead[j] - (near[i] * spread(9 + i, j) + near[i + 1] * spread(10 + i, j))
            rows[k + 1] = part
        far = range(min(k + 3, groups), groups) if groups - k - 3 >= 4 else ()
        for r in range(k + 2, far[0] if far else groups):
            terms = [jnp.broadcast_to(rows[r][:, base + j : base + j + 1], full) * back[j] for j in range(8)]
            while len(terms) > 1:
                terms = [x + y for x, y in zip(terms[::2], terms[1::2])]
            rows[r] = jnp.where(own, 0.0, rows[r]) - terms[0]
        if far:
            mixed = back[0]
            for j in range(1, 8):
                mixed = jnp.where(sub == j, back[j], mixed)
            zero = jnp.zeros(full, jnp.float32)
            hi, lo = split2(jnp.concatenate([zero] * k + [mixed] + [zero] * (groups - k - 1), axis=0))
            delta = jnp.dot(
                left(jnp.concatenate([rows[r] for r in far], axis=0)),
                jnp.concatenate([hi, lo, hi], axis=0),
                preferred_element_type=jnp.float32,
            )
            for i, r in enumerate(far):
                rows[r] = jnp.where(own, 0.0, rows[r]) - delta[i * 8 : i * 8 + 8, :]
        for g in range(8):
            h = g - g % 2
            w = fwd[g] if g == h else fwd[g] - ratio[h] * fwd[h]
            u = fwd_u[g] if g == h else fwd_u[g] - ratio[h] * fwd_u[h]
            u_ref[base + g : base + g + 1, :] = jnp.where(lane >= base + g, u * root[g], 0.0)[:1, :]
            w_ref[base + g : base + g + 1, :] = jnp.where(lane <= base + g, w * root[g], 0.0)[:1, :]


def chol_kernel(place_ref, own_ref, other_ref, x_ref, l_out, o_out, a_ref, l_ref, o_ref, c_ref, u_ref, w_ref, sems):
    n = x_ref.shape[1]
    nb = n // BLOCK
    at = [slice(k * BLOCK, (k + 1) * BLOCK) for k in range(nb)]
    r = lax.broadcasted_iota(jnp.int32, (BLOCK, BLOCK), 0)
    c = lax.broadcasted_iota(jnp.int32, (BLOCK, BLOCK), 1)
    row_scale, col_scale, row_root = [], [], []
    copies = []
    gram = lambda i, j: lower_block(place_ref[2], own_ref, other_ref, i, j)
    for k in range(nb):
        diag = jnp.where(r == c, gram(k, k), 0.0)
        by_row = jnp.broadcast_to(jnp.sum(diag, axis=1, keepdims=True), (BLOCK, BLOCK))
        s = lax.rsqrt(by_row)
        row_scale.append(s)
        row_root.append(by_row * s)
        col_scale.append(lax.rsqrt(jnp.sum(diag, axis=0, keepdims=True)))
    for k in range(nb):
        for i in range(k, nb):
            a_ref[at[i], at[k]] = gram(i, k) * row_scale[i] * col_scale[k]
    for k in range(nb):
        panels = [a_ref[k * BLOCK + p * 8 : k * BLOCK + (p + 1) * 8, at[k]] for p in range(BLOCK // 8)]
        factor_block(panels, c_ref, u_ref.at[k % 2], w_ref.at[k % 2])
        ws = right(w_ref[k % 2])
        below = {}
        for i in range(k + 1, nb):
            below[i] = dot_t(left(a_ref[at[i], at[k]]), ws)
            for j in range(k + 1, i + 1):
                a_ref[at[i], at[j]] = a_ref[at[i], at[j]] - dot_t(left(below[i]), right(below[j]))
        before = x_ref[:, at[k]] * col_scale[k]
        if k:
            before = before - o_ref[:, at[k]]
        solved = dot_t(left(before), ws)
        o_ref[:, at[k]] = solved
        for i in range(k + 1, nb):
            add = dot_t(left(solved), right(below[i]))
            o_ref[:, at[i]] = o_ref[:, at[i]] + add if k else add
        for i in range(k):
            l_ref[at[i], at[k]] = jnp.zeros((BLOCK, BLOCK), jnp.float32)
        l_ref[at[k], at[k]] = u_ref[k % 2].T * row_root[k]
        for i in range(k + 1, nb):
            l_ref[at[i], at[k]] = below[i] * row_root[i]
        copies.append(pltpu.make_async_copy(o_ref.at[:, at[k]], o_out.at[:, at[k]], sems.at[2 * k]))
        copies.append(pltpu.make_async_copy(l_ref.at[:, at[k]], l_out.at[:, at[k]], sems.at[2 * k + 1]))
        copies[-2].start()
        copies[-1].start()
    for copy in copies:
        copy.wait()


def lower_block(core, own_ref, other_ref, i, j):
    half, slot = divmod(LOWER.index((i, j)), len(LOWER) // 2)
    mine = jnp.broadcast_to(core, (8, BLOCK)) == half
    at = slice(slot * 8, slot * 8 + 8)
    parts = [jnp.where(mine, own_ref[chip, at, :], other_ref[chip, at, :]) for chip in range(BLOCK // 8)]
    return jnp.concatenate(parts, axis=0)


def chol_solve(place, own, other, x):
    rows, n = x.shape
    return pl.pallas_call(
        chol_kernel,
        out_shape=(jax.ShapeDtypeStruct((n, n), jnp.float32), jax.ShapeDtypeStruct(x.shape, jnp.float32)),
        in_specs=[SMEM, VMEM, VMEM, VMEM],
        out_specs=[pl.BlockSpec(memory_space=pl.ANY)] * 2,
        scratch_shapes=[
            pltpu.VMEM((n, n), jnp.float32),
            pltpu.VMEM((n, n), jnp.float32),
            pltpu.VMEM((rows, n), jnp.float32),
            pltpu.VMEM((2, 17, 8, BLOCK), jnp.float32),
            pltpu.VMEM((2, BLOCK, BLOCK), jnp.float32),
            pltpu.VMEM((2, BLOCK, BLOCK), jnp.float32),
            pltpu.SemaphoreType.DMA((2 * (n // BLOCK),)),
        ],
        compiler_params=PARAMS,
    )(place, own, other, x)


def gram_kernel(place_ref, p_ref, o_ref, all_ref):
    blocks = all_ref.shape[0] // BLOCK
    half = p_ref.shape[2] // 2
    for chip in range(p_ref.shape[0]):
        for core in range(2):
            all_ref[chip * 32 + core * 16 : chip * 32 + core * 16 + 16, :] = p_ref[chip, :, core * half : (core + 1) * half]
    first = place_ref[1] * 8
    rows = [all_ref[pl.ds(pl.multiple_of(i * BLOCK + first, 8), 8), :] for i in range(blocks)]
    product = dot_t(left(jnp.concatenate(rows, axis=0)), right(all_ref[...]))
    for t, (i, j) in enumerate(LOWER):
        o_ref[t * 8 : t * 8 + 8, :] = product[i * 8 : i * 8 + 8, j * BLOCK : (j + 1) * BLOCK]


def gram_part(columns, place):
    chips, group, depth = columns.shape
    return pl.pallas_call(
        gram_kernel,
        out_shape=jax.ShapeDtypeStruct((8 * len(LOWER), BLOCK), jnp.float32),
        in_specs=[SMEM, VMEM],
        out_specs=VMEM,
        scratch_shapes=[pltpu.VMEM((2 * chips * group, depth // 2), jnp.float32)],
        compiler_params=PARAMS,
    )(place, columns)


def flip_kernel(x_ref, signs_ref, o_ref, buf_ref, row_ref, t_ref, sems):
    rows, n = buf_ref.shape
    parts = rows // BLOCK
    sign_copy = pltpu.make_async_copy(signs_ref, row_ref, sems.at[2 * parts])
    loads, stores = [], []
    for k in range(parts):
        at = pl.ds(k * BLOCK, BLOCK)
        loads.append(pltpu.make_async_copy(x_ref.at[at, :], buf_ref.at[at, :], sems.at[k]))
        stores.append(pltpu.make_async_copy(t_ref.at[:, at], o_ref.at[:, at], sems.at[parts + k]))
    loads[0].start()
    sign_copy.start()
    for load in loads[1:]:
        load.start()
    sign_copy.wait()
    for k in range(parts):
        loads[k].wait()
        at = slice(k * BLOCK, (k + 1) * BLOCK)
        sign = row_ref[:, at].astype(jnp.float32)
        for c in range(n // BLOCK):
            cols = slice(c * BLOCK, (c + 1) * BLOCK)
            t_ref[cols, at] = buf_ref[at, cols].T * sign
        stores[k].start()
    for store in stores:
        store.wait()


def signed_columns(matrix, signs):
    rows, n = matrix.shape
    hbm = pl.BlockSpec(memory_space=pl.ANY)
    return pl.pallas_call(
        flip_kernel,
        out_shape=jax.ShapeDtypeStruct((n, rows), jnp.float32),
        in_specs=[hbm, hbm],
        out_specs=hbm,
        scratch_shapes=[
            pltpu.VMEM((rows, n), jnp.float32),
            pltpu.VMEM((1, rows), jnp.int32),
            pltpu.VMEM((n, rows), jnp.float32),
            pltpu.SemaphoreType.DMA((2 * (rows // BLOCK) + 1,)),
        ],
        compiler_params=WIDE,
    )(matrix, signs.reshape(1, -1))


def signs_of(value, count):
    v = lax.broadcasted_iota(jnp.int32, (count, value.shape[1]), 0) & value
    for shift in (4, 2, 1):
        v = v ^ (v >> shift)
    return (1 - 2 * (v & 1)).astype(jnp.float32)


def mix_kernel(place_ref, x_ref, samples_ref, o_ref, kept_ref, h_ref):
    width = x_ref.shape[0]
    depth = x_ref.shape[1]
    sources = 32
    cols = width // sources
    hi, lo = split2(x_ref[...])
    z_bits = place_ref[0]
    for i in range(kept_ref.shape[0]):
        kept_ref[i] = place_ref[i]
    scale = 1.0 / 512.0
    for c in range(samples_ref.shape[1] // CHUNK):
        s = samples_ref[:, c * CHUNK : (c + 1) * CHUNK]
        within = s & (depth - 1)
        device = s // depth
        low = signs_of(within & 15, 16)
        high = signs_of(within // 16, depth // 16)
        for r in range(depth // 16):
            h_ref[r * 16 : (r + 1) * 16, :] = (low * high[r : r + 1, :]).astype(jnp.bfloat16)
        plane_sign = signs_of((device & 15) | ((device // 256) * 16), sources)
        zv = (device // 16) & z_bits
        zv = zv ^ (zv >> 2)
        zv = zv ^ (zv >> 1)
        z_sign = (1 - 2 * (zv & 1)).astype(jnp.float32) * scale
        h = h_ref[...]
        t = jnp.dot(hi, h, preferred_element_type=jnp.float32)
        t = t + jnp.dot(lo, h, preferred_element_type=jnp.float32)
        acc = t[:cols, :]
        for p in range(1, sources):
            acc = acc + t[p * cols : (p + 1) * cols, :] * plane_sign[p : p + 1, :]
        acc = acc * z_sign
        for b in range(CHUNK // SHARE):
            o_ref[c * (CHUNK // SHARE) + b] = acc[:, b * SHARE : (b + 1) * SHARE]


def sample_columns(columns, samples, place):
    width = columns.shape[0]
    count = samples.shape[0]
    return pl.pallas_call(
        mix_kernel,
        out_shape=(
            jax.ShapeDtypeStruct((count // SHARE, width // 32, SHARE), jnp.float32),
            jax.ShapeDtypeStruct(place.shape, jnp.int32),
        ),
        in_specs=[SMEM, VMEM, VMEM],
        out_specs=[VMEM, SMEM],
        scratch_shapes=[pltpu.VMEM((columns.shape[1], CHUNK), jnp.bfloat16)],
        compiler_params=PARAMS,
    )(place, columns, samples.reshape(1, count))


def near_kernel(x_ref, o_ref):
    half = x_ref.shape[2]
    for core in range(2):
        total = x_ref[core]
        for z in range(1, x_ref.shape[0] // 2):
            total = total + x_ref[2 * z + core]
        o_ref[:, core * half : (core + 1) * half] = total


def near_sum(blocks):
    return pl.pallas_call(
        near_kernel,
        out_shape=jax.ShapeDtypeStruct((blocks.shape[1], 2 * blocks.shape[2]), jnp.float32),
        in_specs=[VMEM],
        out_specs=VMEM,
        compiler_params=PARAMS,
    )(blocks)


def exchange(block, axes):
    return lax.all_to_all(block, axes, 0, 0, tiled=True)


def gather(block, axes):
    count = lax.axis_size(axes)
    return exchange(jnp.broadcast_to(block[None], (count,) + block.shape), axes)


def body(matrix, signs, samples):
    rows, n = matrix.shape
    plane = lax.axis_size(PLANE)
    place = jnp.stack([lax.axis_index(("z_hi", "z_lo")), lax.axis_index(CHIPS), lax.axis_index("core")])
    columns = exchange(signed_columns(matrix, signs).reshape(plane, n // plane, rows), PLANE)
    partial, place = sample_columns(columns.reshape(n, rows), samples, place)
    mine = near_sum(exchange(partial, NEAR))
    mine = jnp.sum(gather(mine, "z_hi"), axis=0)
    every = gather(mine, CHIPS)
    part = gram_part(every, place).reshape(1, 2, 4 * len(LOWER), BLOCK)
    part = jnp.broadcast_to(part, (lax.axis_size("z_lo"),) + part.shape[1:])
    part = jnp.sum(exchange(part.reshape((-1,) + part.shape[2:]), NEAR), axis=0) / jnp.float32(samples.shape[0])
    own = gather(part, CHIPS)
    other = lax.ppermute(own, "core", [(0, 1), (1, 0)])
    return chol_solve(place, own, other, matrix)


def solution(mesh):
    fine = Mesh(mesh.devices.reshape(2, 4, 4, 2, 4, 2), ROW_AXES)
    in_specs = (P(ROW_AXES, None), P(ROW_AXES), P())
    out_specs = (P(), P(ROW_AXES, None))
    return jax.shard_map(body, mesh=fine, in_specs=in_specs, out_specs=out_specs, check_vma=False)
```
